128 devices in a mesh: frame: 32 (over x, z_lo, y), sp: 4 (over z_hi, core).
Axes of the slice: x: 4, y: 4, z: 4 (z_hi: 2, z_lo: 2; z = z_hi * 2 + z_lo), core: 2. Of those that a mesh axis runs over, the one named last changes fastest.
Arguments:
- frames_in: bfloat16 [32, 64, 36, 640], P('frame', 'sp'), may hold values from -6 to 6
- reference_rows: bfloat16 [2304, 640], P(('frame', 'sp')), may hold values from -60 to 60
- norm_conv: float32 [640], replicated, may hold values from 0.1 to 1.9
- conv_weight: bfloat16 [3, 3, 640, 640], replicated, may hold values from -0.078125 to 0.078125
- norm_attn: float32 [640], replicated, may hold values from 0.1 to 1.9
- spatial_qkv: bfloat16 [3, 640, 640], replicated, may hold values from -2 to 2
- spatial_out: bfloat16 [640, 640], replicated, may hold values from -0.25 to 0.25
- time_weight: bfloat16 [3, 640, 640], replicated, may hold values from -0.125 to 0.125
- norm_time: float32 [640], replicated, may hold values from 0.1 to 1.9
- temporal_qkv: bfloat16 [3, 640, 640], replicated, may hold values from -1 to 1
- temporal_out: bfloat16 [640, 640], replicated, may hold values from -0.25 to 0.25
Outputs:
- block_out: bfloat16 [32, 64, 36, 640], P('frame', 'sp')
The draws below stay inside these ranges and needn't reach their ends.
All inputs are finite; a program needn't handle non-finite values.
Results may differ from the reference program's by a relative error of at most 0.018.
Values may be sent and summed in bfloat16 or wider, within the bound.
A program may use at most 128 MiB of HBM per device.

```python
import jax
import jax.numpy as jnp
from jax import lax

C = 640
HEADS = 8
H = 64
W = 36
FRAMES = 32
REF_CELLS = 2304


def draw_reference_rows(key, part):
    key = jax.random.fold_in(key, 11)
    first = jax.random.fold_in(key, 0)
    base = jax.random.normal(first, (REF_CELLS, C), jnp.float32)
    return jnp.clip(base, -6.0, 6.0).astype(jnp.bfloat16)


def draw_frames_in(key, part):
    key = jax.random.fold_in(key, 17)
    first = jax.random.fold_in(key, 0)
    noise = jax.random.normal(first, (FRAMES, H, W, C), jnp.float32)
    return jnp.clip(noise, -6.0, 6.0).astype(jnp.bfloat16)


def draw_spatial_qkv(key, part):
    key = jax.random.fold_in(key, 29)
    base = jnp.clip(jax.random.normal(key, (3, C, C), jnp.float32), -4.0, 4.0) * C ** (-0.5)
    factors = jnp.array([2.5, 1.0, 1.0], jnp.float32)
    return jnp.clip(base * factors[:, None, None], -2.0, 2.0).astype(jnp.bfloat16)


def draw_temporal_qkv(key, part):
    key = jax.random.fold_in(key, 23)
    first = jax.random.fold_in(key, 0)
    base = jnp.clip(jax.random.normal(first, (3, C, C), jnp.float32), -4.0, 4.0) * C ** (-0.5)
    return base.astype(jnp.bfloat16)


def gaussian(stream_key, extent, scale, reach, held_as=jnp.bfloat16):
    entries = jax.random.normal(stream_key, extent, jnp.float32) * scale
    return jnp.minimum(jnp.maximum(entries, -reach), reach).astype(held_as)


def setup_inputs(seed: int = 0) -> dict:
    seeds = jax.random.split(jax.random.key(seed), 12)
    frames_in = draw_frames_in(jax.random.fold_in(seeds[11], 71), 0)
    reference_rows = draw_reference_rows(jax.random.fold_in(seeds[11], 71), 0)
    norm_conv = jnp.clip(1.0 + 0.18 * jax.random.normal(seeds[2], (C,), jnp.float32), 0.1, 1.9)
    conv_weight = gaussian(seeds[3], (3, 3, C, C), (9 * C) ** -0.5, 0.078125)
    norm_attn = jnp.clip(1.0 + 0.18 * jax.random.normal(seeds[4], (C,), jnp.float32), 0.1, 1.9)
    spatial_qkv = draw_spatial_qkv(jax.random.fold_in(seeds[11], 71), 0)
    spatial_out = gaussian(seeds[6], (C, C), C ** -0.5, 0.25)
    time_weight = gaussian(seeds[7], (3, C, C), (3 * C) ** -0.5, 0.125)
    norm_time = jnp.clip(1.0 + 0.18 * jax.random.normal(seeds[8], (C,), jnp.float32), 0.1, 1.9)
    temporal_qkv = draw_temporal_qkv(jax.random.fold_in(seeds[11], 71), 0)
    temporal_out = gaussian(seeds[10], (C, C), C ** -0.5, 0.25)
    return dict(frames_in=frames_in, reference_rows=reference_rows, norm_conv=norm_conv, conv_weight=conv_weight, norm_attn=norm_attn, spatial_qkv=spatial_qkv, spatial_out=spatial_out, time_weight=time_weight, norm_time=norm_time, temporal_qkv=temporal_qkv, temporal_out=temporal_out)


def layer_norm(values, gain):
    mean = lax.optimization_barrier(jnp.mean(values, axis=-1, keepdims=True))
    centred = values - mean
    spread = lax.optimization_barrier(jnp.mean(centred * centred, axis=-1, keepdims=True))
    return centred * lax.rsqrt(spread + 1e-05) * gain.astype(jnp.float32)

def attend(queries, keys, values):
    count, chans = queries.shape
    head_dim = chans // HEADS
    scale = head_dim ** (-0.5)
    query_heads = queries.reshape(count, HEADS, head_dim).transpose(1, 0, 2)
    key_heads = keys.reshape(keys.shape[0], HEADS, head_dim).transpose(1, 0, 2)
    value_heads = values.reshape(values.shape[0], HEADS, head_dim).transpose(1, 0, 2)

    def one_head(pieces):
        query_one, key_one, value_one = pieces
        scores = jnp.dot(query_one, key_one.T, preferred_element_type=jnp.float32) * scale
        largest = lax.optimization_barrier(jnp.max(scores, axis=-1, keepdims=True))
        expon = jnp.exp(scores - largest)
        totals = lax.optimization_barrier(jnp.sum(expon, axis=-1, keepdims=True))
        probs = expon.astype(jnp.bfloat16)
        return jnp.dot(probs, value_one, preferred_element_type=jnp.float32) / totals
    mixed = lax.map(one_head, (query_heads, key_heads, value_heads))
    return mixed.transpose(1, 0, 2).reshape(count, chans).astype(jnp.bfloat16)

def temporal_block(timed_in, norm_time, temporal_qkv, temporal_out):
    frame_count, cell_count, chans = timed_in.shape
    head_dim = chans // HEADS
    scale = head_dim ** (-0.5)
    timed_f = timed_in.astype(jnp.float32)
    tnormed = layer_norm(timed_f, norm_time).astype(jnp.bfloat16).reshape(-1, chans)

    def project(index):
        result = jnp.dot(tnormed, temporal_qkv[index], preferred_element_type=jnp.float32).astype(jnp.bfloat16)
        return result.reshape(frame_count, cell_count, HEADS, head_dim)
    tqueries, tkeys, tvalues = (project(0), project(1), project(2))
    scores = jnp.einsum('frhd,grhd->rhfg', tqueries.astype(jnp.float32), tkeys.astype(jnp.float32)) * scale
    largest = lax.optimization_barrier(jnp.max(scores, axis=-1, keepdims=True))
    expon = jnp.exp(scores - largest)
    totals = lax.optimization_barrier(jnp.sum(expon, axis=-1))
    tprobs = expon.astype(jnp.bfloat16)
    mixed = jnp.einsum('rhfg,grhd->frhd', tprobs.astype(jnp.float32), tvalues.astype(jnp.float32))
    mixed = mixed / totals.transpose(2, 0, 1)[..., None]
    tattended = mixed.astype(jnp.bfloat16).reshape(-1, chans)
    output = timed_f + jnp.dot(tattended, temporal_out, preferred_element_type=jnp.float32).reshape(frame_count, cell_count, chans)
    return output.astype(jnp.bfloat16)

def reference(frames_in, reference_rows, norm_conv, conv_weight, norm_attn, spatial_qkv, spatial_out, time_weight, norm_time, temporal_qkv, temporal_out):
    frame_count = frames_in.shape[0]
    cells = H * W
    inputs = frames_in.astype(jnp.float32)
    activated = jax.nn.silu(layer_norm(inputs, norm_conv)).astype(jnp.bfloat16)
    padded = jnp.pad(activated, ((0, 0), (1, 1), (1, 1), (0, 0)))

    def conv_frame(framepad):
        total = jnp.zeros((cells, C), jnp.float32)
        for row_tap in range(3):
            for col_tap in range(3):
                window = framepad[row_tap:row_tap + H, col_tap:col_tap + W].reshape(cells, C)
                total = total + jnp.dot(window, conv_weight[row_tap, col_tap], preferred_element_type=jnp.float32)
        return total
    convolved = lax.map(conv_frame, padded)
    middle = (inputs.reshape(frame_count, cells, C) + convolved).astype(jnp.bfloat16)
    ref_keys = jnp.dot(reference_rows, spatial_qkv[1], preferred_element_type=jnp.float32).astype(jnp.bfloat16)
    ref_values = jnp.dot(reference_rows, spatial_qkv[2], preferred_element_type=jnp.float32).astype(jnp.bfloat16)

    def spatial_frame(frame_rows):
        normed = layer_norm(frame_rows.astype(jnp.float32), norm_attn).astype(jnp.bfloat16)
        queries = jnp.dot(normed, spatial_qkv[0], preferred_element_type=jnp.float32).astype(jnp.bfloat16)
        keys = jnp.dot(normed, spatial_qkv[1], preferred_element_type=jnp.float32).astype(jnp.bfloat16)
        values = jnp.dot(normed, spatial_qkv[2], preferred_element_type=jnp.float32).astype(jnp.bfloat16)
        keys_all = jnp.concatenate([keys, ref_keys], axis=0)
        values_all = jnp.concatenate([values, ref_values], axis=0)
        attended = attend(queries, keys_all, values_all)
        return (frame_rows.astype(jnp.float32) + jnp.dot(attended, spatial_out, preferred_element_type=jnp.float32)).astype(jnp.bfloat16)
    after = lax.map(spatial_frame, middle)
    padtime = jnp.pad(after, ((1, 1), (0, 0), (0, 0)))
    total = jnp.zeros((frame_count * cells, C), jnp.float32)
    for shift_tap in range(3):
        total = total + jnp.dot(padtime[shift_tap:shift_tap + frame_count].reshape(-1, C), time_weight[shift_tap], preferred_element_type=jnp.float32)
    timed = (after.astype(jnp.float32) + total.reshape(frame_count, cells, C)).astype(jnp.bfloat16)
    output = temporal_block(timed, norm_time, temporal_qkv, temporal_out)
    return output.reshape(frame_count, H, W, C)
```

```python
import functools

import jax
import jax.numpy as jnp
from jax import lax
from jax.experimental import pallas as pl
from jax.experimental.pallas import tpu as pltpu
from jax.sharding import PartitionSpec as P

MESH = pl.DeviceIdType.MESH
BF = jnp.bfloat16
F32 = jnp.float32
C = 640
HEADS = 8
D = 80
MINE = 4
OWN = MINE * D
ROWS = 16
W = 36
PITCH = 40
CELLS = 576
CHIP = 1152
FRAMES = 32
CHUNKS = 3
SLOT = 8
USED = 6
PART = CELLS // CHUNKS
WIDE = FRAMES * SLOT
SCALE = (D ** -0.5) * 1.4426950408889634


def dot(a, b):
    return jnp.dot(a, b, preferred_element_type=F32)


def dot_nt(a, b):
    return lax.dot_general(a, b, (((1,), (1,)), ((), ())), preferred_element_type=F32)


def dot_tn(a, b):
    return lax.dot_general(a, b, (((0,), (0,)), ((), ())), preferred_element_type=F32)


def layer_norm(values, gain):
    mean = jnp.mean(values, axis=-1, keepdims=True)
    centred = values - mean
    spread = jnp.mean(centred * centred, axis=-1, keepdims=True)
    return centred * lax.rsqrt(spread + 1e-05) * gain


def kernel(
    frames, refs, norm_conv, conv_w, norm_attn, sqkv, sout, time_w, norm_time, tqkv, tout,
    out,
    xin, wc, wsq, wso,
    filt, grid, mid,
    rblk, allx, wqt, wvt, wkp, qt, kk, vt, acc, mx, al, s0, s1,
    part, psend, precv,
    asend, arecv, brecv, tgrid, tatt, final, oblk,
    lsem, hs, hr, cs, cr, p1s, p1r, p2s, p2r, xs, xr, ps, pr, a_s, a_r, b_s, b_r,
):
    f = lax.axis_index("frame")
    s = lax.axis_index("sp")
    x = f // 8
    y = f % 4
    z = (s // 2) * 2 + (f // 4) % 2
    core = s % 2
    zc = z * 2 + core

    def dev(px, py, pz, pc):
        px, py, pz = lax.rem(px, 4), lax.rem(py, 4), lax.rem(pz, 4)
        return ((px * 2 + pz % 2) * 4 + py, (pz // 2) * 2 + pc)

    sib = (f, (s // 2) * 2 + 1 - core)
    far = (f, lax.rem(s + 2, 4))

    loads = [
        (frames.at[0], xin.at[pl.ds(1, ROWS)]),
        (refs, rblk.at[zc]),
        (sqkv, wsq),
    ]
    loads += [(conv_w.at[a, b], wc.at[b, pl.ds(a * C, C)]) for b in range(3) for a in range(3)]
    loads += [(sout, wso)]
    loads += [(time_w.at[a], wc.at[0, pl.ds(a * C, C)]) for a in range(3)]
    loads += [(tqkv.at[a], wc.at[1, pl.ds(a * C, C)]) for a in range(3)]
    loads += [(tout, wc.at[2, pl.ds(0, C)])]
    local = [pltpu.make_async_copy(a, b, lsem.at[i]) for i, (a, b) in enumerate(loads)]
    for cp in local[:13]:
        cp.start()

    bar = pltpu.get_barrier_semaphore()
    column = [(dz, dc) for dz in range(4) for dc in range(2) if dz + dc > 0]

    def col_dev(dz, dc):
        return dev(x, y, z + dz, lax.rem(core + dc, 2))

    others = [(dz, dc) for dz, dc in column if not (dz == 0 and dc == 0)]
    for dz, dc in others:
        pl.semaphore_signal(bar, inc=1, device_id=col_dev(dz, dc), device_id_type=MESH)

    def greet(i, _):
        pl.semaphore_signal(
            bar, inc=1, device_id=(lax.rem(f + i, FRAMES), s), device_id_type=MESH
        )
        return 0

    lax.fori_loop(1, FRAMES, greet, 0)
    pl.semaphore_wait(bar, len(others) + FRAMES - 1)

    def remote(src, dst, send, recv, to):
        return pltpu.make_async_remote_copy(
            src_ref=src, dst_ref=dst, send_sem=send, recv_sem=recv, device_id=to, device_id_type=MESH
        )

    up = remote(frames.at[0, 0], xin.at[ROWS + 1], hs.at[0], hr.at[0], (f, jnp.maximum(s - 1, 0)))
    down = remote(frames.at[0, ROWS - 1], xin.at[0], hs.at[1], hr.at[1], (f, jnp.minimum(s + 1, 3)))

    @pl.when(s > 0)
    def _():
        up.start()

    @pl.when(s < 3)
    def _():
        down.start()

    col = [
        remote(refs, rblk.at[zc], cs.at[i], cr.at[i], col_dev(dz, dc))
        for i, (dz, dc) in enumerate(column)
    ]
    for cp in col:
        cp.start()

    local[2].wait()
    pick = (
        lax.broadcasted_iota(jnp.int32, (OWN, C), 1)
        == lax.broadcasted_iota(jnp.int32, (OWN, C), 0) + OWN * core
    ).astype(F32).astype(BF)
    wqt[...] = dot_nt(pick, wsq[0]).astype(BF)
    wvt[...] = dot_nt(pick, wsq[2]).astype(BF)
    lane = lax.broadcasted_iota(jnp.int32, (C, MINE * 128), 1)
    row = lax.broadcasted_iota(jnp.int32, (C, MINE * 128), 0)
    spread = jnp.where(
        jnp.logical_and(lane % 128 < D, row == OWN * core + (lane // 128) * D + lane % 128), 1.0, 0.0
    ).astype(BF)
    wkp[...] = dot(wsq[1], spread).astype(BF)
    vt[:, D:, :] = jnp.where(
        lax.broadcasted_iota(jnp.int32, (MINE, 16, CHIP), 1) == 0, 1.0, 0.0
    ).astype(BF)

    filt[...] = jnp.zeros_like(filt)
    gain_conv = norm_conv[...]

    def activate(k, keep=None):
        v = layer_norm(xin[k].astype(F32), gain_conv)
        v = v / (1.0 + jnp.exp(-v))
        filt[pl.ds(pl.multiple_of(PITCH * k, 8), W), :] = v

    local[0].wait()

    def activate_step(k, _):
        activate(k)
        return 0

    lax.fori_loop(1, ROWS + 1, activate_step, 0)

    local[1].wait()
    for cp in col:
        cp.wait()
    for i in range(8):
        mid[pl.ds(18 * i, 18), :] = rblk[i].astype(F32)
    mine = jnp.int32(1) + x // 2
    allx[mine, lax.rem(x, 2), y] = mid[:144, :].astype(BF)

    def share(first, count):
        return pl.ds(pl.multiple_of(first, 16), count)

    half = share(64 * core, 80)
    home = allx.at[mine, lax.rem(x, 2), y, half]
    p1x = [remote(home, home, p1s.at[i - 1], p1r.at[i - 1], dev(x + i, y, z, core)) for i in (1, 2, 3)]
    p1y = [remote(home, home, p1s.at[i - 1], p1r.at[i - 1], dev(x, y + i, z, core)) for i in (1, 2, 3)]
    line_x = allx.at[pl.ds(1, 2), :, y, half]
    line_y = allx.at[mine, lax.rem(x, 2), :, half]
    p2y = [remote(line_x, line_x, p2s.at[i - 1], p2r.at[i - 1], dev(x, y + i, z, core)) for i in (1, 2, 3)]
    p2x = [remote(line_y, line_y, p2s.at[i - 1], p2r.at[i - 1], dev(x + i, y, z, core)) for i in (1, 2, 3)]

    def by_core(on0, on1, act):
        @pl.when(core == 0)
        def _():
            for cp in on0:
                act(cp)

        @pl.when(core == 1)
        def _():
            for cp in on1:
                act(cp)

    by_core(p1x, p1y, lambda cp: cp.start())

    @pl.when(s > 0)
    def _():
        down.wait_recv()
        activate(0)

    @pl.when(s < 3)
    def _():
        up.wait_recv()
        activate(ROWS + 1)

    @pl.when(s > 0)
    def _():
        up.wait_send()

    @pl.when(s < 3)
    def _():
        down.wait_send()

    def lay(k, _):
        to = pl.ds(pl.multiple_of(80 * k, 16), 80)
        for a in range(3):
            grid[to, a * C : (a + 1) * C] = filt[
                pl.ds(pl.multiple_of(80 * k + PITCH * a, 8), 80), :
            ].astype(BF)
        return 0

    lax.fori_loop(0, 8, lay, 0)
    zero = jnp.zeros((8, C), F32)
    zconv = (s0, s1, filt)
    for i in range(3, 12):
        local[i].wait()
    for b in range(3):
        zconv[b][:8, :C] = zero
        zconv[b][8 + 640 : 16 + 640, :C] = zero
        zconv[b][8 : 8 + 640, :C] = dot(grid[...], wc[b])
        if b == 0:
            by_core(p1x, p1y, lambda cp: cp.wait())
            by_core(p2y, p2x, lambda cp: cp.start())
    for cp in local[13:]:
        cp.start()
    gain_attn = norm_attn[...]
    for k in range(ROWS):
        at = 8 + PITCH * k
        total = (
            s0[at - 1 : at - 1 + W, :C] + s1[at : at + W, :C] + filt[at + 1 : at + 1 + W, :]
        )
        middle = (xin[k + 1].astype(F32) + total).astype(BF).astype(F32)
        mid[W * k : W * k + W, :] = middle
        final[W * k : W * k + W, :] = layer_norm(middle, gain_attn)
    allx[0, 0] = final[...].reshape(4, 144, C).astype(BF)

    to_sib = remote(allx.at[0, 0], allx.at[0, 1], xs.at[0], xr.at[0], sib)
    to_far = remote(allx.at[0, 0], allx.at[3, 0], xs.at[1], xr.at[1], far)
    to_far.start()
    to_sib.start()
    relay = remote(allx.at[3, 0], allx.at[3, 1], xs.at[2], xr.at[2], sib)
    give = allx.at[pl.ds(1, 2), :, :, share(80 * core, 64)]
    ref_swap = remote(give, give, xs.at[3], xr.at[3], sib)

    acc[...] = jnp.zeros_like(acc)
    mx[...] = jnp.full_like(mx, -1e30)
    to_sib.wait_recv()
    qall = dot_nt(wqt[...], allx[0].reshape(CHIP, C)) * SCALE
    qt[...] = qall.astype(BF)

    def scores(h, sref):
        sc = dot(kk[h][:, :D], qt[h * D : (h + 1) * D, :])
        sref[...] = sc
        old = mx[h]
        new = jnp.maximum(old, jnp.max(sc, axis=0, keepdims=True))
        mx[h] = new
        al[h] = jnp.exp2(old - new)

    def weigh(h, sref):
        p = jnp.exp2(sref[...] - mx[h]).astype(BF)
        acc[h] = acc[h] * al[h] + dot(vt[h], p)

    def attend(c, _):
        @pl.when(c == 1)
        def _():
            ref_swap.wait_recv()

        @pl.when(c == 2)
        def _():
            to_far.wait_recv()
            relay.start()

        @pl.when(c == 3)
        def _():
            relay.wait_recv()

        rows = allx[c].reshape(CHIP, C)
        keys = dot(rows, wkp[...])
        vals = dot_nt(wvt[...], rows)
        for h in range(MINE):
            kk[h] = keys[:, h * 128 : (h + 1) * 128].astype(BF)
            vt[h, :D, :] = vals[h * D : (h + 1) * D, :].astype(BF)
        scores(0, s0)
        weigh(0, s0)
        scores(1, s1)
        weigh(1, s1)
        scores(2, s0)

        @pl.when(c == 0)
        def _():
            by_core(p2y, p2x, lambda cp: cp.wait())
            ref_swap.start()

        weigh(2, s0)
        scores(3, s1)
        weigh(3, s1)
        return 0

    lax.fori_loop(0, 4, attend, 0)
    to_sib.wait_send()
    to_far.wait_send()
    relay.wait_send()
    ref_swap.wait_send()
    for i in range(12, len(local)):
        local[i].wait()

    for h in range(MINE):
        qt[h * D : (h + 1) * D, :] = (acc[h, :D, :] / acc[h, D : D + 1, :]).astype(BF)
    wout = wso[pl.ds(pl.multiple_of(OWN * core, 16), OWN), :]
    part[...] = dot_tn(qt[...], wout)
    psend[...] = part[CELLS:, :].astype(BF)
    swaps = [
        remote(
            psend.at[pl.ds(PART * j, PART)], precv.at[pl.ds(PART * j, PART)], ps.at[j], pr.at[j], sib
        )
        for j in range(CHUNKS)
    ]
    for cp in swaps:
        cp.start()

    wide_row = lax.broadcasted_iota(jnp.int32, (WIDE, PART), 0)
    part_row = lax.broadcasted_iota(jnp.int32, (WIDE, PART), 1)
    fan = jnp.where(
        jnp.logical_and(wide_row % SLOT < USED, part_row == (wide_row // SLOT) * USED + wide_row % SLOT),
        1.0, 0.0,
    ).astype(BF)

    def to_all(src, dst, send, recv, j):
        def go(i, _):
            peer = lax.rem(f + i, FRAMES)
            remote(src.at[j, peer], dst.at[j, f], send.at[j, peer], recv.at[j, f], (peer, s)).start()
            return 0

        lax.fori_loop(1, FRAMES, go, 0)
        dst[j, f] = src[j, f]

    def from_all(src, dst, send, recv, j):
        def go(i, _):
            peer = lax.rem(f + i, FRAMES)
            remote(src.at[j, peer], dst.at[j, peer], send.at[j, peer], recv.at[j, peer], (peer, s)).wait()
            return 0

        lax.fori_loop(1, FRAMES, go, 0)

    def depart(j, _):
        @pl.when(j == 0)
        def _():
            swaps[0].wait()

        @pl.when(j == 1)
        def _():
            swaps[1].wait()

        @pl.when(j == 2)
        def _():
            swaps[2].wait()

        at = pl.ds(pl.multiple_of(PART * j, 16), PART)
        after = (mid[at, :] + part[at, :] + precv[at, :].astype(F32)).astype(BF)
        asend[j] = dot(fan, after).reshape(FRAMES, SLOT, C).astype(BF)
        to_all(asend, arecv, a_s, a_r, j)
        return 0

    lax.fori_loop(0, CHUNKS, depart, 0)

    gain_time = norm_time[...]
    same = (
        lax.broadcasted_iota(jnp.int32, (WIDE, WIDE), 0) % SLOT
        == lax.broadcasted_iota(jnp.int32, (WIDE, WIDE), 1) % SLOT
    )
    def through_time(j, _):
        from_all(asend, arecv, a_s, a_r, j)
        block = arecv[j].astype(F32).reshape(WIDE, C)
        tgrid[:, :C] = jnp.concatenate([zero, block[:-SLOT]], axis=0).astype(BF)
        tgrid[:, C : 2 * C] = block.astype(BF)
        tgrid[:, 2 * C :] = jnp.concatenate([block[SLOT:], zero], axis=0).astype(BF)
        timed = (block + dot(tgrid[...], wc[0])).astype(BF).astype(F32)
        tn = layer_norm(timed, gain_time).astype(BF)
        q = (dot(tn, wc[1, 0 * C : 1 * C, :]) * SCALE).astype(BF)
        k = dot(tn, wc[1, 1 * C : 2 * C, :]).astype(BF)
        v = dot(tn, wc[1, 2 * C : 3 * C, :]).astype(BF)
        for h in range(HEADS):
            lo, hi = (h * D) // 128 * 128, -(-((h + 1) * D) // 128) * 128
            ln = lax.broadcasted_iota(jnp.int32, (1, hi - lo), 1) + lo
            inside = jnp.logical_and(ln >= h * D, ln < (h + 1) * D)
            qh = q[:, lo:hi] * jnp.where(inside, 1.0, 0.0).astype(BF)
            sc = jnp.where(same, dot_nt(qh, k[:, lo:hi]), -1e30)
            e = jnp.exp2(sc - jnp.max(sc, axis=1, keepdims=True))
            total = jnp.sum(e, axis=1, keepdims=True)
            o = dot(e.astype(BF), v[:, lo:hi]) / total
            if h == 0:
                tatt[:, lo:hi] = o
            else:
                tatt[:, lo:hi] = jnp.where(inside, o, tatt[:, lo:hi])
        res = timed + dot(tatt[...].astype(BF), wc[2, :C, :])
        asend[j] = res.reshape(FRAMES, SLOT, C).astype(BF)
        to_all(asend, brecv, b_s, b_r, j)
        return 0

    lax.fori_loop(0, CHUNKS, through_time, 0)

    def arrive(j, _):
        from_all(asend, brecv, b_s, b_r, j)
        got = brecv[j].astype(F32).reshape(WIDE, C).astype(BF)
        final[pl.ds(pl.multiple_of(PART * j, 16), PART), :] = dot_tn(fan, got)
        return 0

    lax.fori_loop(0, CHUNKS, arrive, 0)
    for k in range(ROWS):
        oblk[k] = final[W * k : W * k + W, :].astype(BF)
    done = pltpu.make_async_copy(oblk, out.at[0], lsem.at[0])
    done.start()
    done.wait()


def block(
    frames_in, reference_rows, norm_conv, conv_weight, norm_attn, spatial_qkv, spatial_out,
    time_weight, norm_time, temporal_qkv, temporal_out,
):
    hbm = pl.BlockSpec(memory_space=pl.ANY)
    vm = pl.BlockSpec(memory_space=pltpu.VMEM)
    v = pltpu.VMEM
    dma = pltpu.SemaphoreType.DMA
    scratch = [
        v((ROWS + 2, W, C), BF), v((3, 3 * C, C), BF), v((3, C, C), BF), v((C, C), BF),
        v((18 * PITCH, C), F32), v((640, 3 * C), BF), v((CELLS, C), F32),
        v((8, 18, C), BF), v((4, 2, 4, 144, C), BF), v((OWN, C), BF), v((OWN, C), BF),
        v((C, MINE * 128), BF), v((OWN, CHIP), BF), v((MINE, CHIP, 128), BF), v((MINE, 96, CHIP), BF),
        v((MINE, 96, CHIP), F32), v((MINE, 1, CHIP), F32), v((MINE, 1, CHIP), F32),
        v((CHIP, CHIP), F32), v((CHIP, CHIP), F32),
        v((CHIP, C), F32), v((CELLS, C), BF), v((CELLS, C), BF),
        v((CHUNKS, FRAMES, SLOT, C), BF), v((CHUNKS, FRAMES, SLOT, C), BF),
        v((CHUNKS, FRAMES, SLOT, C), BF),
        v((WIDE, 3 * C), BF), v((WIDE, C), F32), v((CELLS, C), F32), v((ROWS, W, C), BF),
        dma((20,)), dma((2,)), dma((2,)), dma((7,)), dma((7,)),
        dma((3,)), dma((3,)), dma((3,)), dma((3,)), dma((4,)), dma((4,)), dma((3,)), dma((3,)),
        dma((CHUNKS, FRAMES)), dma((CHUNKS, FRAMES)), dma((CHUNKS, FRAMES)), dma((CHUNKS, FRAMES)),
    ]
    return pl.pallas_call(
        kernel,
        out_shape=jax.ShapeDtypeStruct(frames_in.shape, BF),
        in_specs=[hbm, hbm, vm, hbm, vm, hbm, hbm, hbm, vm, hbm, hbm],
        out_specs=hbm,
        scratch_shapes=scratch,
        compiler_params=pltpu.CompilerParams(
            collective_id=0, has_side_effects=True, vmem_limit_bytes=62 * 2**20
        ),
    )(
        frames_in, reference_rows, norm_conv.reshape(1, C), conv_weight, norm_attn.reshape(1, C),
        spatial_qkv, spatial_out, time_weight, norm_time.reshape(1, C), temporal_qkv, temporal_out,
    )


def solution(mesh):
    rep = P()
    in_specs = (P("frame", "sp", None, None), P(("frame", "sp"), None)) + (rep,) * 9
    return jax.shard_map(
        block, mesh=mesh, in_specs=in_specs, out_specs=P("frame", "sp", None, None), check_vma=False
    )
```

```python
import functools

import jax
import jax.numpy as jnp
from jax import lax
from jax.experimental import pallas as pl
from jax.experimental.pallas import tpu as pltpu
from jax.sharding import PartitionSpec as P

MESH = pl.DeviceIdType.MESH
BF = jnp.bfloat16
F32 = jnp.float32
C = 640
HEADS = 8
D = 80
MINE = 4
OWN = MINE * D
ROWS = 16
W = 36
CELLS = 576
CHIP = 1152
FRAMES = 32
SLOT = 8
WIDE = FRAMES * SLOT
PARTS = ((0, 256), (256, 256), (512, 64))
CHUNKS = len(PARTS)
LAST = PARTS[2][1]
SCALE = (D ** -0.5) * 1.4426950408889634


def dot(a, b):
    return jnp.dot(a, b, preferred_element_type=F32)


def dot_nt(a, b):
    return lax.dot_general(a, b, (((1,), (1,)), ((), ())), preferred_element_type=F32)


def dot_tn(a, b):
    return lax.dot_general(a, b, (((0,), (0,)), ((), ())), preferred_element_type=F32)


def layer_norm(values, gain):
    mean = jnp.mean(values, axis=-1, keepdims=True)
    centred = values - mean
    spread = jnp.mean(centred * centred, axis=-1, keepdims=True)
    return centred * lax.rsqrt(spread + 1e-05) * gain


def kernel(
    frames, refs, norm_conv, conv_w, norm_attn, sqkv, sout, time_w, norm_time, tqkv, tout,
    out,
    xin, wc, wsq, wso,
    rims, rimr, grid, mid,
    rblk, allx, wqt, wvt, wkp, qt, kk, vt, acc, mx, al, s0, s1,
    part, psend, precv,
    asend, arecv, brecv, tgrid, tatt, oblk,
    lsem, hs, hr, cs, cr, p1s, p1r, p2s, p2r, xs, xr, ps, pr, a_s, a_r, b_s, b_r,
):
    f = lax.axis_index("frame")
    s = lax.axis_index("sp")
    x = f // 8
    y = f % 4
    z = (s // 2) * 2 + (f // 4) % 2
    core = s % 2
    zc = z * 2 + core

    def dev(px, py, pz, pc):
        px, py, pz = lax.rem(px, 4), lax.rem(py, 4), lax.rem(pz, 4)
        return ((px * 2 + pz % 2) * 4 + py, (pz // 2) * 2 + pc)

    sib = (f, (s // 2) * 2 + 1 - core)
    far = (f, lax.rem(s + 2, 4))

    loads = [
        (frames, xin),
        (refs, rblk.at[zc]),
        (sqkv, wsq),
    ]
    loads += [(conv_w.at[a, b], wc.at[b, pl.ds(a * C, C)]) for b in range(3) for a in range(3)]
    loads += [(sout, wso)]
    loads += [(time_w.at[a], wc.at[0, pl.ds(a * C, C)]) for a in range(3)]
    loads += [(tqkv.at[a], wc.at[1, pl.ds(a * C, C)]) for a in range(3)]
    loads += [(tout, wc.at[2, pl.ds(0, C)])]
    local = [pltpu.make_async_copy(a, b, lsem.at[i]) for i, (a, b) in enumerate(loads)]
    for cp in local[:13]:
        cp.start()

    bar = pltpu.get_barrier_semaphore()
    column = [(dz, dc) for dz in range(4) for dc in range(2) if dz + dc > 0]

    def col_dev(dz, dc):
        return dev(x, y, z + dz, lax.rem(core + dc, 2))

    others = [(dz, dc) for dz, dc in column if not (dz == 0 and dc == 0)]
    for dz, dc in others:
        pl.semaphore_signal(bar, inc=1, device_id=col_dev(dz, dc), device_id_type=MESH)

    for i in (1, 2, 3):
        pl.semaphore_signal(bar, inc=1, device_id=dev(x + i, y, z, core), device_id_type=MESH)
        pl.semaphore_signal(bar, inc=1, device_id=dev(x, y + i, z, core), device_id_type=MESH)

    local[0].wait()
    rim_row = lax.broadcasted_iota(jnp.int32, (96, CELLS), 0)
    rim_cell = lax.broadcasted_iota(jnp.int32, (96, CELLS), 1)
    rim = jnp.where(
        rim_cell == jnp.where(rim_row < 48, rim_row * ROWS, (rim_row - 48) * ROWS + ROWS - 1), 1.0, 0.0
    ).astype(BF)
    rims[...] = dot(rim, xin[...]).astype(BF)

    local[2].wait()
    pick = (
        lax.broadcasted_iota(jnp.int32, (OWN, C), 1)
        == lax.broadcasted_iota(jnp.int32, (OWN, C), 0) + OWN * core
    ).astype(F32).astype(BF)
    wqt[...] = dot_nt(pick, wsq[0]).astype(BF)
    wvt[...] = dot_nt(pick, wsq[2]).astype(BF)
    lane = lax.broadcasted_iota(jnp.int32, (C, MINE * 128), 1)
    row = lax.broadcasted_iota(jnp.int32, (C, MINE * 128), 0)
    spread = jnp.where(
        jnp.logical_and(lane % 128 < D, row == OWN * core + (lane // 128) * D + lane % 128), 1.0, 0.0
    ).astype(BF)
    wkp[...] = dot(wsq[1], spread).astype(BF)
    vt[:, D:, :] = jnp.where(
        lax.broadcasted_iota(jnp.int32, (MINE, 16, CHIP), 1) == 0, 1.0, 0.0
    ).astype(BF)

    def remote(src, dst, send, recv, to):
        return pltpu.make_async_remote_copy(
            src_ref=src, dst_ref=dst, send_sem=send, recv_sem=recv, device_id=to, device_id_type=MESH
        )

    gain_conv = norm_conv[...].reshape(1, C)

    def activated(v):
        v = layer_norm(v.astype(F32), gain_conv)
        return v / (1.0 + jnp.exp(-v))

    nothing = jnp.zeros((8, C), F32)

    def activate(k, _):
        v = activated(xin[pl.ds(pl.multiple_of(64 * k, 16), 64), :])
        for i in range(4):
            at = pl.multiple_of(128 * k + 32 * i, 8)
            part[pl.ds(at, 8), :] = nothing
            part[pl.ds(at + 8, ROWS), :] = v[ROWS * i : ROWS * (i + 1)]
            part[pl.ds(at + 24, 8), :] = nothing
        return 0

    lax.fori_loop(0, CELLS // 64, activate, 0)

    grid[:ROWS, :] = jnp.zeros((ROWS, 3 * C), BF)
    grid[CELLS + ROWS :, :] = jnp.zeros((ROWS, 3 * C), BF)
    for k in range(W):
        for a in range(3):
            grid[ROWS * (k + 1) : ROWS * (k + 2), a * C : (a + 1) * C] = part[
                32 * k + 7 + a : 32 * k + 7 + a + ROWS, :
            ].astype(BF)
    for i in range(3, 12):
        local[i].wait()

    def conv_tap(b):
        return dot(grid[ROWS * b : ROWS * b + CELLS, :], wc[b])

    pl.semaphore_wait(bar, 13)
    up = remote(
        rims.at[pl.ds(0, 48)], rimr.at[pl.ds(48, 48)], hs.at[0], hr.at[0], (f, jnp.maximum(s - 1, 0))
    )
    down = remote(
        rims.at[pl.ds(48, 48)], rimr.at[pl.ds(0, 48)], hs.at[1], hr.at[1], (f, jnp.minimum(s + 1, 3))
    )

    @pl.when(s > 0)
    def _():
        up.start()

    @pl.when(s < 3)
    def _():
        down.start()

    col = [
        remote(rblk.at[zc], rblk.at[zc], cs.at[i], cr.at[i], col_dev(dz, dc))
        for i, (dz, dc) in enumerate(column)
    ]
    local[1].wait()
    for cp in col:
        cp.start()


    mid[...] = conv_tap(0)
    mid[...] += conv_tap(1)
    mid[...] += conv_tap(2)

    def patch(tap, first, values):
        rim = activated(values).astype(BF)
        for b in range(3):
            part[64 * b : 64 * b + 8, :] = nothing
            part[64 * b + 8 : 64 * b + 56, :] = dot(rim, wc[b, tap * C : (tap + 1) * C, :])
        part[192 : 192 + W, :] = part[7 : 7 + W, :] + part[72 : 72 + W, :] + part[137 : 137 + W, :]
        for k in range(W):
            mid[ROWS * k + first : ROWS * k + first + 1, :] += part[192 + k : 193 + k, :]

    @pl.when(s > 0)
    def _():
        down.wait_recv()
        patch(0, 0, rimr[:48])

    @pl.when(s < 3)
    def _():
        up.wait_recv()
        patch(2, ROWS - 1, rimr[48:])

    @pl.when(s > 0)
    def _():
        up.wait_send()

    @pl.when(s < 3)
    def _():
        down.wait_send()

    for cp in local[13:]:
        cp.start()
    gain_attn = norm_attn[...].reshape(1, C)

    def settle(k, _):
        at = pl.ds(pl.multiple_of(144 * k, 16), 144)
        middle = (xin[at, :].astype(F32) + mid[at, :]).astype(BF).astype(F32)
        mid[at, :] = middle
        allx[0, 0, k] = layer_norm(middle, gain_attn).astype(BF)
        return 0

    lax.fori_loop(0, 4, settle, 0)

    to_sib = remote(allx.at[0, 0], allx.at[0, 1], xs.at[0], xr.at[0], sib)
    to_far = remote(allx.at[0, 0], allx.at[3, 0], xs.at[1], xr.at[1], far)
    to_far.start()
    for cp in col:
        cp.wait()
    for i in range(8):
        tatt[pl.ds(18 * i, 18), :] = rblk[i].astype(F32)
    mine = jnp.int32(1) + x // 2
    allx[mine, lax.rem(x, 2), y] = tatt[:144, :].astype(BF)


    def share(first, count):
        return pl.ds(pl.multiple_of(first, 16), count)

    half = share(64 * core, 80)

    def line_one(i):
        return dev(x + i * (1 - core), y + i * core, z, core)

    def line_two(i):
        return dev(x + i * core, y + i * (1 - core), z, core)

    def home(i):
        px, py = lax.rem(x + 4 - i * (1 - core), 4), lax.rem(y + 4 - i * core, 4)
        return allx.at[1 + px // 2, lax.rem(px, 2), py, half]

    p1 = [remote(home(0), home(0), p1s.at[i - 1], p1r.at[i - 1], line_one(i)) for i in (1, 2, 3)]
    p2 = [
        [
            remote(home(k), home(k), p2s.at[k, i - 1], p2r.at[k, i - 1], line_two(i))
            for i in (1, 2, 3)
        ]
        for k in range(4)
    ]
    for cp in p1 + p2[0]:
        cp.start()
    to_sib.start()

    relay = remote(allx.at[3, 0], allx.at[3, 1], xs.at[2], xr.at[2], sib)
    ref_swap = [
        remote(
            allx.at[k, :, :, share(80 * core, 64)], allx.at[k, :, :, share(80 * core, 64)],
            xs.at[2 + k], xr.at[2 + k], sib,
        )
        for k in (1, 2)
    ]

    acc[...] = jnp.zeros_like(acc)
    mx[...] = jnp.full_like(mx, -1e30)
    to_sib.wait_recv()
    own, next_door = allx[0, 0].reshape(CELLS, C), allx[0, 1].reshape(CELLS, C)
    asking = jnp.concatenate(
        [cells[lo : lo + n] for lo, n in PARTS for cells in (own, next_door)], axis=0
    )
    qall = dot_nt(wqt[...], asking) * SCALE
    qt[...] = qall.astype(BF)
    for i in range(3):
        p1[i].wait()
        for cp in p2[i + 1]:
            cp.start()

    def scores(h, sref, lo=0, n=CHIP):
        at = slice(lo, lo + n)
        sc = dot(kk[h][:, :D], qt[h * D : (h + 1) * D, at])
        sref[:, :n] = sc
        old = mx[h, :, at]
        new = jnp.maximum(old, jnp.max(sc, axis=0, keepdims=True))
        mx[h, :, at] = new
        al[h, :, at] = jnp.exp2(old - new)

    def weigh(h, sref, lo=0, n=CHIP):
        at = slice(lo, lo + n)
        p = jnp.exp2(sref[:, :n] - mx[h, :, at]).astype(BF)
        acc[h, :, at] = acc[h, :, at] * al[h, :, at] + dot(vt[h], p)

    def project(c):
        rows = allx[c].reshape(CHIP, C)
        keys = dot(rows, wkp[...])
        vals = dot_nt(wvt[...], rows)
        for h in range(MINE):
            kk[h] = keys[:, h * 128 : (h + 1) * 128].astype(BF)
            vt[h, :D, :] = vals[h * D : (h + 1) * D, :].astype(BF)

    def attend(c, _):
        @pl.when(c == 1)
        def _():
            ref_swap[0].wait_recv()

        @pl.when(c == 2)
        def _():
            ref_swap[1].wait_recv()
            to_far.wait_recv()
            relay.start()

        project(c)
        scores(0, s0)
        weigh(0, s0)
        scores(1, s1)
        weigh(1, s1)
        scores(2, s0)

        weigh(2, s0)
        scores(3, s1)
        weigh(3, s1)

        @pl.when(c == 0)
        def _():
            for line in p2:
                for cp in line:
                    cp.wait()
            for cp in ref_swap:
                cp.start()

        return 0

    lax.fori_loop(0, 3, attend, 0)
    relay.wait_recv()
    project(3)
    local[12].wait()
    wout = wso[pl.ds(pl.multiple_of(OWN * core, 16), OWN), :]
    swaps = [
        remote(psend.at[pl.ds(lo, n)], precv.at[pl.ds(lo, n)], ps.at[j], pr.at[j], sib)
        for j, (lo, n) in enumerate(PARTS)
    ]
    wide_row = lax.broadcasted_iota(jnp.int32, (WIDE, LAST), 0)
    last_row = lax.broadcasted_iota(jnp.int32, (WIDE, LAST), 1)
    few = LAST // FRAMES
    fan = jnp.where(
        jnp.logical_and(wide_row % SLOT < few, last_row == (wide_row // SLOT) * few + wide_row % SLOT),
        1.0, 0.0,
    ).astype(BF)

    def to_all(src, dst, send, recv, j):
        def go(i, _):
            peer = lax.rem(f + i, FRAMES)
            remote(src.at[j, peer], dst.at[j, f], send.at[j], recv.at[j], (peer, s)).start()
            return 0

        lax.fori_loop(1, FRAMES, go, 0)
        dst[j, f] = src[j, f]

    def from_all(src, dst, send, recv, j):
        every = pl.ds(0, FRAMES - 1)
        remote(src.at[j, every], dst.at[j, every], send.at[j], recv.at[j], sib).wait()

    def out_project(j):
        lo, n = PARTS[j]
        at = slice(2 * lo, 2 * lo + 2 * n)
        for h in range(MINE):
            qt[h * D : (h + 1) * D, at] = (acc[h, :D, at] / acc[h, D : D + 1, at]).astype(BF)
        part[at, :] = dot_tn(qt[:, at], wout)
        psend[lo : lo + n, :] = part[2 * lo + n : 2 * lo + 2 * n, :].astype(BF)
        swaps[j].start()

    def depart(j):
        lo, n = PARTS[j]
        swaps[j].wait()
        at = slice(lo, lo + n)
        after = mid[at, :] + part[2 * lo : 2 * lo + n, :] + precv[at, :].astype(F32)
        if n < WIDE:
            after = dot(fan, after.astype(BF))
        asend[j] = after.reshape(FRAMES, SLOT, C).astype(BF)
        to_all(asend, arecv, a_s, a_r, j)

    items = [(j, h) for j in range(CHUNKS) for h in range(MINE)]

    def span(j):
        return 2 * PARTS[j][0], 2 * PARTS[j][1]

    scores(0, s0, *span(0))
    for i, (j, h) in enumerate(items):
        weigh(h, (s0, s1)[i % 2], *span(j))
        if i + 1 < len(items):
            jn, hn = items[i + 1]
            scores(hn, (s0, s1)[(i + 1) % 2], *span(jn))
        if h == MINE - 1:
            out_project(j)
        if j > 0 and h == 1:
            depart(j - 1)
    for i in range(13, len(local)):
        local[i].wait()
    depart(CHUNKS - 1)

    to_sib.wait_send()
    to_far.wait_send()
    relay.wait_send()
    for cp in ref_swap:
        cp.wait_send()

    gain_time = norm_time[...].reshape(1, C)
    zero = jnp.zeros((SLOT, C), F32)
    same = (
        lax.broadcasted_iota(jnp.int32, (WIDE, WIDE), 0) % SLOT
        == lax.broadcasted_iota(jnp.int32, (WIDE, WIDE), 1) % SLOT
    )
    def through_time(j, _):
        from_all(asend, arecv, a_s, a_r, j)
        block = arecv[j].astype(F32).reshape(WIDE, C)
        tgrid[:, :C] = jnp.concatenate([zero, block[:-SLOT]], axis=0).astype(BF)
        tgrid[:, C : 2 * C] = block.astype(BF)
        tgrid[:, 2 * C :] = jnp.concatenate([block[SLOT:], zero], axis=0).astype(BF)
        timed = (block + dot(tgrid[...], wc[0])).astype(BF).astype(F32)
        tn = layer_norm(timed, gain_time).astype(BF)
        q = (dot(tn, wc[1, 0 * C : 1 * C, :]) * SCALE).astype(BF)
        k = dot(tn, wc[1, 1 * C : 2 * C, :]).astype(BF)
        v = dot(tn, wc[1, 2 * C : 3 * C, :]).astype(BF)
        for h in range(HEADS):
            lo, hi = (h * D) // 128 * 128, -(-((h + 1) * D) // 128) * 128
            ln = lax.broadcasted_iota(jnp.int32, (1, hi - lo), 1) + lo
            inside = jnp.logical_and(ln >= h * D, ln < (h + 1) * D)
            qh = q[:, lo:hi] * jnp.where(inside, 1.0, 0.0).astype(BF)
            sc = jnp.where(same, dot_nt(qh, k[:, lo:hi]), -1e30)
            e = jnp.exp2(sc - jnp.max(sc, axis=1, keepdims=True))
            total = jnp.sum(e, axis=1, keepdims=True)
            o = dot(e.astype(BF), v[:, lo:hi]) / total
            if h == 0:
                tatt[:, lo:hi] = o
            else:
                tatt[:, lo:hi] = jnp.where(inside, o, tatt[:, lo:hi])
        res = timed + dot(tatt[...].astype(BF), wc[2, :C, :])
        asend[j] = res.reshape(FRAMES, SLOT, C).astype(BF)
        to_all(asend, brecv, b_s, b_r, j)
        return 0

    lax.fori_loop(0, CHUNKS, through_time, 0)

    for j, (lo, n) in enumerate(PARTS):
        from_all(asend, brecv, b_s, b_r, j)
        got = brecv[j].astype(F32).reshape(WIDE, C)
        if n < WIDE:
            got = dot_tn(fan, got.astype(BF))
        oblk[lo : lo + n, :] = got.astype(BF)
    done = pltpu.make_async_copy(oblk, out, lsem.at[0])
    done.start()
    done.wait()


def block(
    frames_in, reference_rows, norm_conv, conv_weight, norm_attn, spatial_qkv, spatial_out,
    time_weight, norm_time, temporal_qkv, temporal_out,
):
    hbm = pl.BlockSpec(memory_space=pl.ANY)
    vm = pl.BlockSpec(memory_space=pltpu.VMEM)
    v = pltpu.VMEM
    dma = pltpu.SemaphoreType.DMA
    scratch = [
        v((CELLS, C), BF), v((3, 3 * C, C), BF), v((3, C, C), BF), v((C, C), BF),
        v((96, C), BF), v((96, C), BF), v((CELLS + 2 * ROWS, 3 * C), BF), v((CELLS, C), F32),
        v((8, 18, C), BF), v((4, 2, 4, 144, C), BF), v((OWN, C), BF), v((OWN, C), BF),
        v((C, MINE * 128), BF), v((OWN, CHIP), BF), v((MINE, CHIP, 128), BF), v((MINE, 96, CHIP), BF),
        v((MINE, 96, CHIP), F32), v((MINE, 1, CHIP), F32), v((MINE, 1, CHIP), F32),
        v((CHIP, CHIP), F32), v((CHIP, CHIP), F32),
        v((CHIP, C), F32), v((CELLS, C), BF), v((CELLS, C), BF),
        v((CHUNKS, FRAMES, SLOT, C), BF), v((CHUNKS, FRAMES, SLOT, C), BF),
        v((CHUNKS, FRAMES, SLOT, C), BF),
        v((WIDE, 3 * C), BF), v((WIDE, C), F32), v((CELLS, C), BF),
        dma((20,)), dma((2,)), dma((2,)), dma((7,)), dma((7,)),
        dma((3,)), dma((3,)), dma((4, 3)), dma((4, 3)), dma((5,)), dma((5,)), dma((3,)), dma((3,)),
        dma((CHUNKS,)), dma((CHUNKS,)), dma((CHUNKS,)), dma((CHUNKS,)),
    ]
    cells = frames_in.transpose(0, 2, 1, 3).reshape(CELLS, C)
    res = pl.pallas_call(
        kernel,
        out_shape=jax.ShapeDtypeStruct((CELLS, C), BF),
        in_specs=[hbm, hbm, vm, hbm, vm, hbm, hbm, hbm, vm, hbm, hbm],
        out_specs=hbm,
        scratch_shapes=scratch,
        compiler_params=pltpu.CompilerParams(
            collective_id=0, has_side_effects=True, vmem_limit_bytes=62 * 2**20
        ),
    )(
        cells, reference_rows, norm_conv, conv_weight, norm_attn, spatial_qkv, spatial_out,
        time_weight, norm_time, temporal_qkv, temporal_out,
    )
    return res.reshape(1, W, ROWS, C).transpose(0, 2, 1, 3)


def solution(mesh):
    rep = P()
    in_specs = (P("frame", "sp", None, None), P(("frame", "sp"), None)) + (rep,) * 9
    return jax.shard_map(
        block, mesh=mesh, in_specs=in_specs, out_specs=P("frame", "sp", None, None), check_vma=False
    )
```

```python
import functools

import jax
import jax.numpy as jnp
from jax import lax
from jax.experimental import pallas as pl
from jax.experimental.pallas import tpu as pltpu
from jax.sharding import PartitionSpec as P

MESH = pl.DeviceIdType.MESH
BF = jnp.bfloat16
F32 = jnp.float32
C = 640
HEADS = 8
D = 80
MINE = 4
OWN = MINE * D
ROWS = 16
W = 36
CELLS = 576
CHIP = 1152
FRAMES = 32
SLOT = 8
WIDE = FRAMES * SLOT
PARTS = ((0, 256), (256, 256), (512, 64))
CHUNKS = len(PARTS)
LAST = PARTS[2][1]
SCALE = (D ** -0.5) * 1.4426950408889634


def dot(a, b):
    return jnp.dot(a, b, preferred_element_type=F32)


def dot_nt(a, b):
    return lax.dot_general(a, b, (((1,), (1,)), ((), ())), preferred_element_type=F32)


def dot_tn(a, b):
    return lax.dot_general(a, b, (((0,), (0,)), ((), ())), preferred_element_type=F32)


def layer_norm(values, gain):
    mean = jnp.mean(values, axis=-1, keepdims=True)
    centred = values - mean
    spread = jnp.mean(centred * centred, axis=-1, keepdims=True)
    return centred * lax.rsqrt(spread + 1e-05) * gain


def kernel(
    frames, refs, norm_conv, conv_w, norm_attn, sqkv, sout, time_w, norm_time, tqkv, tout,
    out,
    xin, wc, wsq, wso,
    rims, rimr, grid, mid,
    rblk, allx, wqt, wvt, wkp, qt, kk, vt, acc, mx, al, s0, s1,
    part, psend, precv,
    asend, arecv, brecv, tgrid, tatt, oblk,
    lsem, hs, hr, cs, cr, p1s, p1r, p2s, p2r, xs, xr, ps, pr, a_s, a_r, b_s, b_r,
):
    f = lax.axis_index("frame")
    s = lax.axis_index("sp")
    x = f // 8
    y = f % 4
    z = (s // 2) * 2 + (f // 4) % 2
    core = s % 2
    zc = z * 2 + core

    def dev(px, py, pz, pc):
        px, py, pz = lax.rem(px, 4), lax.rem(py, 4), lax.rem(pz, 4)
        return ((px * 2 + pz % 2) * 4 + py, (pz // 2) * 2 + pc)

    sib = (f, (s // 2) * 2 + 1 - core)
    far = (f, lax.rem(s + 2, 4))

    loads = [
        (frames, xin),
        (refs, rblk.at[zc]),
        (sqkv, wsq),
    ]
    loads += [(conv_w.at[a, b], wc.at[b, pl.ds(a * C, C)]) for b in range(3) for a in range(3)]
    loads += [(sout, wso)]
    loads += [(time_w.at[a], wc.at[0, pl.ds(a * C, C)]) for a in range(3)]
    loads += [(tqkv.at[a], wc.at[1, pl.ds(a * C, C)]) for a in range(3)]
    loads += [(tout, wc.at[2, pl.ds(0, C)])]
    local = [pltpu.make_async_copy(a, b, lsem.at[i]) for i, (a, b) in enumerate(loads)]
    for cp in local[:13]:
        cp.start()

    bar = pltpu.get_barrier_semaphore()
    column = [(dz, dc) for dz in range(4) for dc in range(2) if dz + dc > 0]

    def col_dev(dz, dc):
        return dev(x, y, z + dz, lax.rem(core + dc, 2))

    others = [(dz, dc) for dz, dc in column if not (dz == 0 and dc == 0)]
    for dz, dc in others:
        pl.semaphore_signal(bar, inc=1, device_id=col_dev(dz, dc), device_id_type=MESH)

    for i in (1, 2, 3):
        pl.semaphore_signal(bar, inc=1, device_id=dev(x + i, y, z, core), device_id_type=MESH)
        pl.semaphore_signal(bar, inc=1, device_id=dev(x, y + i, z, core), device_id_type=MESH)

    local[0].wait()
    rim_row = lax.broadcasted_iota(jnp.int32, (96, CELLS), 0)
    rim_cell = lax.broadcasted_iota(jnp.int32, (96, CELLS), 1)
    rim = jnp.where(
        rim_cell == jnp.where(rim_row < 48, rim_row * ROWS, (rim_row - 48) * ROWS + ROWS - 1), 1.0, 0.0
    ).astype(BF)
    rims[...] = dot(rim, xin[...]).astype(BF)

    local[2].wait()
    pick = (
        lax.broadcasted_iota(jnp.int32, (OWN, C), 1)
        == lax.broadcasted_iota(jnp.int32, (OWN, C), 0) + OWN * core
    ).astype(F32).astype(BF)
    wqt[...] = dot_nt(pick, wsq[0]).astype(BF)
    wvt[...] = dot_nt(pick, wsq[2]).astype(BF)
    lane = lax.broadcasted_iota(jnp.int32, (C, MINE * 128), 1)
    row = lax.broadcasted_iota(jnp.int32, (C, MINE * 128), 0)
    spread = jnp.where(
        jnp.logical_and(lane % 128 < D, row == OWN * core + (lane // 128) * D + lane % 128), 1.0, 0.0
    ).astype(BF)
    wkp[...] = dot(wsq[1], spread).astype(BF)
    vt[:, D:, :] = jnp.where(
        lax.broadcasted_iota(jnp.int32, (MINE, 16, CHIP), 1) == 0, 1.0, 0.0
    ).astype(BF)

    def remote(src, dst, send, recv, to):
        return pltpu.make_async_remote_copy(
            src_ref=src, dst_ref=dst, send_sem=send, recv_sem=recv, device_id=to, device_id_type=MESH
        )

    gain_conv = norm_conv[...].reshape(1, C)

    def activated(v):
        v = layer_norm(v.astype(F32), gain_conv)
        return v / (1.0 + jnp.exp(-v))

    nothing = jnp.zeros((8, C), F32)

    def activate(k, _):
        v = activated(xin[pl.ds(pl.multiple_of(64 * k, 16), 64), :])
        for i in range(4):
            at = pl.multiple_of(128 * k + 32 * i, 8)
            part[pl.ds(at, 8), :] = nothing
            part[pl.ds(at + 8, ROWS), :] = v[ROWS * i : ROWS * (i + 1)]
            part[pl.ds(at + 24, 8), :] = nothing
        return 0

    lax.fori_loop(0, CELLS // 64, activate, 0)

    grid[:ROWS, :] = jnp.zeros((ROWS, 3 * C), BF)
    grid[CELLS + ROWS :, :] = jnp.zeros((ROWS, 3 * C), BF)
    for k in range(W):
        for a in range(3):
            grid[ROWS * (k + 1) : ROWS * (k + 2), a * C : (a + 1) * C] = part[
                32 * k + 7 + a : 32 * k + 7 + a + ROWS, :
            ].astype(BF)
    for i in range(3, 12):
        local[i].wait()

    def conv_tap(b):
        return dot(grid[ROWS * b : ROWS * b + CELLS, :], wc[b])

    pl.semaphore_wait(bar, 13)
    up = remote(
        rims.at[pl.ds(0, 48)], rimr.at[pl.ds(48, 48)], hs.at[0], hr.at[0], (f, jnp.maximum(s - 1, 0))
    )
    down = remote(
        rims.at[pl.ds(48, 48)], rimr.at[pl.ds(0, 48)], hs.at[1], hr.at[1], (f, jnp.minimum(s + 1, 3))
    )

    @pl.when(s > 0)
    def _():
        up.start()

    @pl.when(s < 3)
    def _():
        down.start()

    col = [
        remote(rblk.at[zc], rblk.at[zc], cs.at[i], cr.at[i], col_dev(dz, dc))
        for i, (dz, dc) in enumerate(column)
    ]
    local[1].wait()
    for cp in col:
        cp.start()


    mid[...] = conv_tap(0)
    mid[...] += conv_tap(1)
    mid[...] += conv_tap(2)

    for cp in col:
        cp.wait()
    for i in range(8):
        tatt[pl.ds(18 * i, 18), :] = rblk[i].astype(F32)
    mine = jnp.int32(1) + x // 2
    allx[mine, lax.rem(x, 2), y] = tatt[:144, :].astype(BF)


    def share(first, count):
        return pl.ds(pl.multiple_of(first, 16), count)

    half = share(64 * core, 80)

    def line_one(i):
        return dev(x + i * (1 - core), y + i * core, z, core)

    def line_two(i):
        return dev(x + i * core, y + i * (1 - core), z, core)

    def home(i):
        px, py = lax.rem(x + 4 - i * (1 - core), 4), lax.rem(y + 4 - i * core, 4)
        return allx.at[1 + px // 2, lax.rem(px, 2), py, half]

    p1 = [remote(home(0), home(0), p1s.at[i - 1], p1r.at[i - 1], line_one(i)) for i in (1, 2, 3)]
    p2 = [
        [
            remote(home(k), home(k), p2s.at[k, i - 1], p2r.at[k, i - 1], line_two(i))
            for i in (1, 2, 3)
        ]
        for k in range(4)
    ]
    for cp in p1 + p2[0]:
        cp.start()

    def patch(tap, first, values):
        rim = activated(values).astype(BF)
        for b in range(3):
            part[64 * b : 64 * b + 8, :] = nothing
            part[64 * b + 8 : 64 * b + 56, :] = dot(rim, wc[b, tap * C : (tap + 1) * C, :])
        part[192 : 192 + W, :] = part[7 : 7 + W, :] + part[72 : 72 + W, :] + part[137 : 137 + W, :]
        for k in range(W):
            mid[ROWS * k + first : ROWS * k + first + 1, :] += part[192 + k : 193 + k, :]

    @pl.when(s > 0)
    def _():
        down.wait_recv()
        patch(0, 0, rimr[:48])

    @pl.when(s < 3)
    def _():
        up.wait_recv()
        patch(2, ROWS - 1, rimr[48:])

    @pl.when(s > 0)
    def _():
        up.wait_send()

    @pl.when(s < 3)
    def _():
        down.wait_send()

    for cp in local[13:]:
        cp.start()
    gain_attn = norm_attn[...].reshape(1, C)

    def settle(k, _):
        at = pl.ds(pl.multiple_of(144 * k, 16), 144)
        middle = (xin[at, :].astype(F32) + mid[at, :]).astype(BF).astype(F32)
        mid[at, :] = middle
        allx[0, 0, k] = layer_norm(middle, gain_attn).astype(BF)
        return 0

    lax.fori_loop(0, 4, settle, 0)

    to_sib = remote(allx.at[0, 0], allx.at[0, 1], xs.at[0], xr.at[0], sib)
    to_far = remote(allx.at[0, 0], allx.at[3, 0], xs.at[1], xr.at[1], far)
    to_far.start()
    to_sib.start()
    relay = remote(allx.at[3, 0], allx.at[3, 1], xs.at[2], xr.at[2], sib)
    ref_swap = [
        remote(
            allx.at[k, :, :, share(80 * core, 64)], allx.at[k, :, :, share(80 * core, 64)],
            xs.at[2 + k], xr.at[2 + k], sib,
        )
        for k in (1, 2)
    ]

    acc[...] = jnp.zeros_like(acc)
    mx[...] = jnp.full_like(mx, -1e30)
    to_sib.wait_recv()
    own, next_door = allx[0, 0].reshape(CELLS, C), allx[0, 1].reshape(CELLS, C)
    asking = jnp.concatenate(
        [cells[lo : lo + n] for lo, n in PARTS for cells in (own, next_door)], axis=0
    )
    qall = dot_nt(wqt[...], asking) * SCALE
    qt[...] = qall.astype(BF)
    for i in range(3):
        p1[i].wait()
        for cp in p2[i + 1]:
            cp.start()

    def scores(h, sref, lo=0, n=CHIP):
        at = slice(lo, lo + n)
        sc = dot(kk[h][:, :D], qt[h * D : (h + 1) * D, at])
        sref[:, :n] = sc
        old = mx[h, :, at]
        new = jnp.maximum(old, jnp.max(sc, axis=0, keepdims=True))
        mx[h, :, at] = new
        al[h, :, at] = jnp.exp2(old - new)

    def weigh(h, sref, lo=0, n=CHIP):
        at = slice(lo, lo + n)
        p = jnp.exp2(sref[:, :n] - mx[h, :, at]).astype(BF)
        acc[h, :, at] = acc[h, :, at] * al[h, :, at] + dot(vt[h], p)

    def project(c):
        rows = allx[c].reshape(CHIP, C)
        keys = dot(rows, wkp[...])
        vals = dot_nt(wvt[...], rows)
        for h in range(MINE):
            kk[h] = keys[:, h * 128 : (h + 1) * 128].astype(BF)
            vt[h, :D, :] = vals[h * D : (h + 1) * D, :].astype(BF)

    def attend(c, _):
        @pl.when(c == 1)
        def _():
            ref_swap[0].wait_recv()

        @pl.when(c == 2)
        def _():
            ref_swap[1].wait_recv()
            to_far.wait_recv()
            relay.start()

        project(c)
        scores(0, s0)
        weigh(0, s0)
        scores(1, s1)
        weigh(1, s1)
        scores(2, s0)

        weigh(2, s0)
        scores(3, s1)
        weigh(3, s1)

        @pl.when(c == 0)
        def _():
            for line in p2:
                for cp in line:
                    cp.wait()
            for cp in ref_swap:
                cp.start()

        return 0

    lax.fori_loop(0, 3, attend, 0)
    relay.wait_recv()
    project(3)
    local[12].wait()
    wout = wso[pl.ds(pl.multiple_of(OWN * core, 16), OWN), :]
    swaps = [
        remote(psend.at[pl.ds(lo, n)], precv.at[pl.ds(lo, n)], ps.at[j], pr.at[j], sib)
        for j, (lo, n) in enumerate(PARTS)
    ]
    wide_row = lax.broadcasted_iota(jnp.int32, (WIDE, LAST), 0)
    last_row = lax.broadcasted_iota(jnp.int32, (WIDE, LAST), 1)
    few = LAST // FRAMES
    fan = jnp.where(
        jnp.logical_and(wide_row % SLOT < few, last_row == (wide_row // SLOT) * few + wide_row % SLOT),
        1.0, 0.0,
    ).astype(BF)

    hops = sorted(
        ((dx, dz, dy) for dx in range(4) for dz in range(2) for dy in range(4) if dx + dz + dy),
        key=lambda d: -(min(d[0], 4 - d[0]) + d[1] + min(d[2], 4 - d[2])),
    )
    zl = (f // 4) % 2
    rounds = [lax.rem(x + dx, 4) * 8 + lax.rem(zl + dz, 2) * 4 + lax.rem(y + dy, 4) for dx, dz, dy in hops]

    def to_all(src, dst, send, recv, j):
        for peer in rounds:
            remote(src.at[j, peer], dst.at[j, f], send.at[j], recv.at[j], (peer, s)).start()
        dst[j, f] = src[j, f]

    def from_all(src, dst, send, recv, j):
        every = pl.ds(0, FRAMES - 1)
        remote(src.at[j, every], dst.at[j, every], send.at[j], recv.at[j], sib).wait()

    def out_project(j):
        lo, n = PARTS[j]
        at = slice(2 * lo, 2 * lo + 2 * n)
        for h in range(MINE):
            qt[h * D : (h + 1) * D, at] = (acc[h, :D, at] / acc[h, D : D + 1, at]).astype(BF)
        part[at, :] = dot_tn(qt[:, at], wout)
        psend[lo : lo + n, :] = part[2 * lo + n : 2 * lo + 2 * n, :].astype(BF)
        swaps[j].start()

    def depart(j):
        lo, n = PARTS[j]
        swaps[j].wait()
        at = slice(lo, lo + n)
        after = mid[at, :] + part[2 * lo : 2 * lo + n, :] + precv[at, :].astype(F32)
        if n < WIDE:
            after = dot(fan, after.astype(BF))
        asend[j] = after.reshape(FRAMES, SLOT, C).astype(BF)
        to_all(asend, arecv, a_s, a_r, j)

    items = [(j, h) for j in range(CHUNKS) for h in range(MINE)]

    def span(j):
        return 2 * PARTS[j][0], 2 * PARTS[j][1]

    scores(0, s0, *span(0))
    for i, (j, h) in enumerate(items):
        weigh(h, (s0, s1)[i % 2], *span(j))
        if i + 1 < len(items):
            jn, hn = items[i + 1]
            scores(hn, (s0, s1)[(i + 1) % 2], *span(jn))
        if h == MINE - 1:
            out_project(j)
        if j > 0 and h == 1:
            depart(j - 1)
    for i in range(13, len(local)):
        local[i].wait()
    depart(CHUNKS - 1)

    to_sib.wait_send()
    to_far.wait_send()
    relay.wait_send()
    for cp in ref_swap:
        cp.wait_send()

    gain_time = norm_time[...].reshape(1, C)
    zero = jnp.zeros((SLOT, C), F32)
    def same_cell(n, cells):
        return (
            lax.broadcasted_iota(jnp.int32, (n, n), 0) % cells
            == lax.broadcasted_iota(jnp.int32, (n, n), 1) % cells
        )

    def through_time(block, n, same):
        timed = (block + dot(tgrid[:n, :], wc[0])).astype(BF).astype(F32)
        tn = layer_norm(timed, gain_time).astype(BF)
        q = (dot(tn, wc[1, 0 * C : 1 * C, :]) * SCALE).astype(BF)
        k = dot(tn, wc[1, 1 * C : 2 * C, :]).astype(BF)
        v = dot(tn, wc[1, 2 * C : 3 * C, :]).astype(BF)
        for h in range(HEADS):
            lo, hi = (h * D) // 128 * 128, -(-((h + 1) * D) // 128) * 128
            ln = lax.broadcasted_iota(jnp.int32, (1, hi - lo), 1) + lo
            inside = jnp.logical_and(ln >= h * D, ln < (h + 1) * D)
            qh = q[:, lo:hi] * jnp.where(inside, 1.0, 0.0).astype(BF)
            sc = jnp.where(same, dot_nt(qh, k[:, lo:hi]), -1e30)
            e = jnp.exp2(sc - jnp.max(sc, axis=1, keepdims=True))
            total = jnp.sum(e, axis=1, keepdims=True)
            o = dot(e.astype(BF), v[:, lo:hi]) / total
            if h == 0:
                tatt[:n, lo:hi] = o
            else:
                tatt[:n, lo:hi] = jnp.where(inside, o, tatt[:n, lo:hi])
        return timed + dot(tatt[:n, :].astype(BF), wc[2, :C, :])

    all_rows = same_cell(WIDE, SLOT)

    def full_part(j, _):
        from_all(asend, arecv, a_s, a_r, j)
        block = arecv[j].astype(F32).reshape(WIDE, C)
        tgrid[:, :C] = jnp.concatenate([zero, block[:-SLOT]], axis=0).astype(BF)
        tgrid[:, C : 2 * C] = block.astype(BF)
        tgrid[:, 2 * C :] = jnp.concatenate([block[SLOT:], zero], axis=0).astype(BF)
        res = through_time(block, WIDE, all_rows)
        asend[j] = res.reshape(FRAMES, SLOT, C).astype(BF)
        to_all(asend, brecv, b_s, b_r, j)
        return 0

    lax.fori_loop(0, CHUNKS - 1, full_part, 0)

    last = CHUNKS - 1
    at_row = lax.broadcasted_iota(jnp.int32, (LAST, WIDE), 0)
    from_row = lax.broadcasted_iota(jnp.int32, (LAST, WIDE), 1)
    from_all(asend, arecv, a_s, a_r, last)
    wide = arecv[last].astype(F32).reshape(WIDE, C).astype(BF)
    drawn = [
        dot(
            jnp.where(
                from_row == (at_row // few + t - 1) * SLOT + at_row % few, 1.0, 0.0
            ).astype(BF),
            wide,
        )
        for t in range(3)
    ]
    for t in range(3):
        tgrid[:LAST, t * C : (t + 1) * C] = drawn[t].astype(BF)
    res = through_time(drawn[1], LAST, same_cell(LAST, few))
    asend[last] = dot(fan, res.astype(BF)).reshape(FRAMES, SLOT, C).astype(BF)
    to_all(asend, brecv, b_s, b_r, last)

    done = [
        pltpu.make_async_copy(oblk.at[pl.ds(lo, n)], out.at[pl.ds(lo, n)], lsem.at[j])
        for j, (lo, n) in enumerate(PARTS)
    ]
    for j, (lo, n) in enumerate(PARTS):
        from_all(asend, brecv, b_s, b_r, j)
        got = brecv[j].astype(F32).reshape(WIDE, C)
        if n < WIDE:
            got = dot_tn(fan, got.astype(BF))
        oblk[lo : lo + n, :] = got.astype(BF)
        done[j].start()
    for cp in done:
        cp.wait()


def block(
    frames_in, reference_rows, norm_conv, conv_weight, norm_attn, spatial_qkv, spatial_out,
    time_weight, norm_time, temporal_qkv, temporal_out,
):
    hbm = pl.BlockSpec(memory_space=pl.ANY)
    vm = pl.BlockSpec(memory_space=pltpu.VMEM)
    v = pltpu.VMEM
    dma = pltpu.SemaphoreType.DMA
    scratch = [
        v((CELLS, C), BF), v((3, 3 * C, C), BF), v((3, C, C), BF), v((C, C), BF),
        v((96, C), BF), v((96, C), BF), v((CELLS + 2 * ROWS, 3 * C), BF), v((CELLS, C), F32),
        v((8, 18, C), BF), v((4, 2, 4, 144, C), BF), v((OWN, C), BF), v((OWN, C), BF),
        v((C, MINE * 128), BF), v((OWN, CHIP), BF), v((MINE, CHIP, 128), BF), v((MINE, 96, CHIP), BF),
        v((MINE, 96, CHIP), F32), v((MINE, 1, CHIP), F32), v((MINE, 1, CHIP), F32),
        v((CHIP, CHIP), F32), v((CHIP, CHIP), F32),
        v((CHIP, C), F32), v((CELLS, C), BF), v((CELLS, C), BF),
        v((CHUNKS, FRAMES, SLOT, C), BF), v((CHUNKS, FRAMES, SLOT, C), BF),
        v((CHUNKS, FRAMES, SLOT, C), BF),
        v((WIDE, 3 * C), BF), v((WIDE, C), F32), v((CELLS, C), BF),
        dma((20,)), dma((2,)), dma((2,)), dma((7,)), dma((7,)),
        dma((3,)), dma((3,)), dma((4, 3)), dma((4, 3)), dma((5,)), dma((5,)), dma((3,)), dma((3,)),
        dma((CHUNKS,)), dma((CHUNKS,)), dma((CHUNKS,)), dma((CHUNKS,)),
    ]
    cells = frames_in.transpose(0, 2, 1, 3).reshape(CELLS, C)
    res = pl.pallas_call(
        kernel,
        out_shape=jax.ShapeDtypeStruct((CELLS, C), BF),
        in_specs=[hbm, hbm, vm, hbm, vm, hbm, hbm, hbm, vm, hbm, hbm],
        out_specs=hbm,
        scratch_shapes=scratch,
        compiler_params=pltpu.CompilerParams(
            collective_id=0, has_side_effects=True, vmem_limit_bytes=62 * 2**20
        ),
    )(
        cells, reference_rows, norm_conv, conv_weight, norm_attn, spatial_qkv, spatial_out,
        time_weight, norm_time, temporal_qkv, temporal_out,
    )
    return res.reshape(1, W, ROWS, C).transpose(0, 2, 1, 3)


def solution(mesh):
    rep = P()
    in_specs = (P("frame", "sp", None, None), P(("frame", "sp"), None)) + (rep,) * 9
    return jax.shard_map(
        block, mesh=mesh, in_specs=in_specs, out_specs=P("frame", "sp", None, None), check_vma=False
    )
```

```python
import functools

import jax
import jax.numpy as jnp
from jax import lax
from jax.experimental import pallas as pl
from jax.experimental.pallas import tpu as pltpu
from jax.sharding import PartitionSpec as P

MESH = pl.DeviceIdType.MESH
BF = jnp.bfloat16
F32 = jnp.float32
C = 640
HEADS = 8
D = 80
MINE = 4
OWN = MINE * D
ROWS = 16
W = 36
CELLS = 576
CHIP = 1152
FRAMES = 32
SLOT = 8
WIDE = FRAMES * SLOT
PARTS = ((0, 256), (256, 256), (512, 64))
CHUNKS = len(PARTS)
LAST = PARTS[2][1]
SCALE = (D ** -0.5) * 1.4426950408889634


def dot(a, b):
    return jnp.dot(a, b, preferred_element_type=F32)


def dot_nt(a, b):
    return lax.dot_general(a, b, (((1,), (1,)), ((), ())), preferred_element_type=F32)


def dot_tn(a, b):
    return lax.dot_general(a, b, (((0,), (0,)), ((), ())), preferred_element_type=F32)


def layer_norm(values, gain):
    mean = jnp.mean(values, axis=-1, keepdims=True)
    centred = values - mean
    spread = jnp.mean(centred * centred, axis=-1, keepdims=True)
    return centred * lax.rsqrt(spread + 1e-05) * gain


def kernel(
    frames, refs, norm_conv, conv_w, norm_attn, sqkv, sout, time_w, norm_time, tqkv, tout,
    out,
    xin, wc, wsq, wso,
    rims, rimr, grid, mid,
    rblk, allx, wqt, wvt, wkp, qt, kk, vt, acc, mx, al, s0, s1,
    part, psend, precv,
    asend, arecv, brecv, lsend, lrecv, lback, tgrid, tatt, oblk,
    lsem, hs, hr, cs, cr, p1s, p1r, p2s, p2r, xs, xr, ps, pr, a_s, a_r, b_s, b_r,
):
    f = lax.axis_index("frame")
    s = lax.axis_index("sp")
    x = f // 8
    y = f % 4
    z = (s // 2) * 2 + (f // 4) % 2
    core = s % 2
    zc = z * 2 + core

    def dev(px, py, pz, pc):
        px, py, pz = lax.rem(px, 4), lax.rem(py, 4), lax.rem(pz, 4)
        return ((px * 2 + pz % 2) * 4 + py, (pz // 2) * 2 + pc)

    sib = (f, (s // 2) * 2 + 1 - core)
    far = (f, lax.rem(s + 2, 4))

    loads = [
        (frames, xin),
        (refs, rblk.at[zc]),
        (sqkv, wsq),
    ]
    loads += [(conv_w.at[a, b], wc.at[b, pl.ds(a * C, C)]) for b in range(3) for a in range(3)]
    loads += [(sout, wso)]
    loads += [(time_w.at[a], wc.at[0, pl.ds(a * C, C)]) for a in range(3)]
    loads += [(tqkv.at[a], wc.at[1, pl.ds(a * C, C)]) for a in range(3)]
    loads += [(tout, wc.at[2, pl.ds(0, C)])]
    local = [pltpu.make_async_copy(a, b, lsem.at[i]) for i, (a, b) in enumerate(loads)]
    for cp in local[:13]:
        cp.start()

    bar = pltpu.get_barrier_semaphore()
    column = [(dz, dc) for dz in range(4) for dc in range(2) if dz + dc > 0]

    def col_dev(dz, dc):
        return dev(x, y, z + dz, lax.rem(core + dc, 2))

    others = [(dz, dc) for dz, dc in column if not (dz == 0 and dc == 0)]
    for dz, dc in others:
        pl.semaphore_signal(bar, inc=1, device_id=col_dev(dz, dc), device_id_type=MESH)

    for i in (1, 2, 3):
        pl.semaphore_signal(bar, inc=1, device_id=dev(x + i, y, z, core), device_id_type=MESH)
        pl.semaphore_signal(bar, inc=1, device_id=dev(x, y + i, z, core), device_id_type=MESH)

    local[0].wait()
    rim_row = lax.broadcasted_iota(jnp.int32, (96, CELLS), 0)
    rim_cell = lax.broadcasted_iota(jnp.int32, (96, CELLS), 1)
    rim = jnp.where(
        rim_cell == jnp.where(rim_row < 48, rim_row * ROWS, (rim_row - 48) * ROWS + ROWS - 1), 1.0, 0.0
    ).astype(BF)
    rims[...] = dot(rim, xin[...]).astype(BF)

    local[2].wait()
    pick = (
        lax.broadcasted_iota(jnp.int32, (OWN, C), 1)
        == lax.broadcasted_iota(jnp.int32, (OWN, C), 0) + OWN * core
    ).astype(F32).astype(BF)
    wqt[...] = dot_nt(pick, wsq[0]).astype(BF)
    wvt[...] = dot_nt(pick, wsq[2]).astype(BF)
    lane = lax.broadcasted_iota(jnp.int32, (C, MINE * 128), 1)
    row = lax.broadcasted_iota(jnp.int32, (C, MINE * 128), 0)
    spread = jnp.where(
        jnp.logical_and(lane % 128 < D, row == OWN * core + (lane // 128) * D + lane % 128), 1.0, 0.0
    ).astype(BF)
    wkp[...] = dot(wsq[1], spread).astype(BF)
    vt[:, D:, :] = jnp.where(
        lax.broadcasted_iota(jnp.int32, (MINE, 16, CHIP), 1) == 0, 1.0, 0.0
    ).astype(BF)

    def remote(src, dst, send, recv, to):
        return pltpu.make_async_remote_copy(
            src_ref=src, dst_ref=dst, send_sem=send, recv_sem=recv, device_id=to, device_id_type=MESH
        )

    gain_conv = norm_conv[...].reshape(1, C)

    def activated(v):
        v = layer_norm(v.astype(F32), gain_conv)
        return v / (1.0 + jnp.exp(-v))

    nothing = jnp.zeros((8, C), F32)

    def activate(k, _):
        v = activated(xin[pl.ds(pl.multiple_of(64 * k, 16), 64), :])
        for i in range(4):
            at = pl.multiple_of(128 * k + 32 * i, 8)
            part[pl.ds(at, 8), :] = nothing
            part[pl.ds(at + 8, ROWS), :] = v[ROWS * i : ROWS * (i + 1)]
            part[pl.ds(at + 24, 8), :] = nothing
        return 0

    lax.fori_loop(0, CELLS // 64, activate, 0)

    grid[:ROWS, :] = jnp.zeros((ROWS, 3 * C), BF)
    grid[CELLS + ROWS :, :] = jnp.zeros((ROWS, 3 * C), BF)
    for k in range(W):
        for a in range(3):
            grid[ROWS * (k + 1) : ROWS * (k + 2), a * C : (a + 1) * C] = part[
                32 * k + 7 + a : 32 * k + 7 + a + ROWS, :
            ].astype(BF)
    for i in range(3, 12):
        local[i].wait()

    def conv_tap(b):
        return dot(grid[ROWS * b : ROWS * b + CELLS, :], wc[b])

    pl.semaphore_wait(bar, 13)
    up = remote(
        rims.at[pl.ds(0, 48)], rimr.at[pl.ds(48, 48)], hs.at[0], hr.at[0], (f, jnp.maximum(s - 1, 0))
    )
    down = remote(
        rims.at[pl.ds(48, 48)], rimr.at[pl.ds(0, 48)], hs.at[1], hr.at[1], (f, jnp.minimum(s + 1, 3))
    )

    @pl.when(s > 0)
    def _():
        up.start()

    @pl.when(s < 3)
    def _():
        down.start()

    col = [
        remote(rblk.at[zc], rblk.at[zc], cs.at[i], cr.at[i], col_dev(dz, dc))
        for i, (dz, dc) in enumerate(column)
    ]
    local[1].wait()
    for cp in col:
        cp.start()


    mid[...] = conv_tap(0)
    mid[...] += conv_tap(1)
    mid[...] += conv_tap(2)

    for cp in col:
        cp.wait()
    for i in range(8):
        tatt[pl.ds(18 * i, 18), :] = rblk[i].astype(F32)
    mine = jnp.int32(1) + x // 2
    allx[mine, lax.rem(x, 2), y] = tatt[:144, :].astype(BF)


    def share(first, count):
        return pl.ds(pl.multiple_of(first, 16), count)

    half = share(64 * core, 80)

    def line_one(i):
        return dev(x + i * (1 - core), y + i * core, z, core)

    def line_two(i):
        return dev(x + i * core, y + i * (1 - core), z, core)

    def home(i):
        px, py = lax.rem(x + 4 - i * (1 - core), 4), lax.rem(y + 4 - i * core, 4)
        return allx.at[1 + px // 2, lax.rem(px, 2), py, half]

    p1 = [remote(home(0), home(0), p1s.at[i - 1], p1r.at[i - 1], line_one(i)) for i in (1, 2, 3)]
    p2 = [
        [
            remote(home(k), home(k), p2s.at[k, i - 1], p2r.at[k, i - 1], line_two(i))
            for i in (1, 2, 3)
        ]
        for k in range(4)
    ]
    for cp in p1 + p2[0]:
        cp.start()

    def patch(tap, first, values):
        rim = activated(values).astype(BF)
        for b in range(3):
            part[64 * b : 64 * b + 8, :] = nothing
            part[64 * b + 8 : 64 * b + 56, :] = dot(rim, wc[b, tap * C : (tap + 1) * C, :])
        part[192 : 192 + W, :] = part[7 : 7 + W, :] + part[72 : 72 + W, :] + part[137 : 137 + W, :]
        for k in range(W):
            mid[ROWS * k + first : ROWS * k + first + 1, :] += part[192 + k : 193 + k, :]

    @pl.when(s > 0)
    def _():
        down.wait_recv()
        patch(0, 0, rimr[:48])

    @pl.when(s < 3)
    def _():
        up.wait_recv()
        patch(2, ROWS - 1, rimr[48:])

    @pl.when(s > 0)
    def _():
        up.wait_send()

    @pl.when(s < 3)
    def _():
        down.wait_send()

    for cp in local[13:]:
        cp.start()
    gain_attn = norm_attn[...].reshape(1, C)

    def settle(k, _):
        at = pl.ds(pl.multiple_of(144 * k, 16), 144)
        middle = (xin[at, :].astype(F32) + mid[at, :]).astype(BF).astype(F32)
        mid[at, :] = middle
        allx[0, 0, k] = layer_norm(middle, gain_attn).astype(BF)
        return 0

    lax.fori_loop(0, 4, settle, 0)

    to_sib = remote(allx.at[0, 0], allx.at[0, 1], xs.at[0], xr.at[0], sib)
    to_far = remote(allx.at[0, 0], allx.at[3, 0], xs.at[1], xr.at[1], far)
    to_far.start()
    to_sib.start()
    relay = remote(allx.at[3, 0], allx.at[3, 1], xs.at[2], xr.at[2], sib)
    ref_swap = [
        remote(
            allx.at[k, :, :, share(80 * core, 64)], allx.at[k, :, :, share(80 * core, 64)],
            xs.at[2 + k], xr.at[2 + k], sib,
        )
        for k in (1, 2)
    ]

    acc[...] = jnp.zeros_like(acc)
    mx[...] = jnp.full_like(mx, -1e30)
    to_sib.wait_recv()
    own, next_door = allx[0, 0].reshape(CELLS, C), allx[0, 1].reshape(CELLS, C)
    asking = jnp.concatenate(
        [cells[lo : lo + n] for lo, n in PARTS for cells in (own, next_door)], axis=0
    )
    qall = dot_nt(wqt[...], asking) * SCALE
    qt[...] = qall.astype(BF)
    for i in range(3):
        p1[i].wait()
        for cp in p2[i + 1]:
            cp.start()

    def scores(h, sref, lo=0, n=CHIP):
        at = slice(lo, lo + n)
        sc = dot(kk[h][:, :D], qt[h * D : (h + 1) * D, at])
        sref[:, :n] = sc
        old = mx[h, :, at]
        new = jnp.maximum(old, jnp.max(sc, axis=0, keepdims=True))
        mx[h, :, at] = new
        al[h, :, at] = jnp.exp2(old - new)

    def weigh(h, sref, lo=0, n=CHIP):
        at = slice(lo, lo + n)
        p = jnp.exp2(sref[:, :n] - mx[h, :, at]).astype(BF)
        acc[h, :, at] = acc[h, :, at] * al[h, :, at] + dot(vt[h], p)

    def project(c):
        rows = allx[c].reshape(CHIP, C)
        keys = dot(rows, wkp[...])
        vals = dot_nt(wvt[...], rows)
        for h in range(MINE):
            kk[h] = keys[:, h * 128 : (h + 1) * 128].astype(BF)
            vt[h, :D, :] = vals[h * D : (h + 1) * D, :].astype(BF)

    def attend(c, _):
        @pl.when(c == 1)
        def _():
            ref_swap[0].wait_recv()

        @pl.when(c == 2)
        def _():
            ref_swap[1].wait_recv()
            to_far.wait_recv()
            relay.start()

        project(c)
        scores(0, s0)
        weigh(0, s0)
        scores(1, s1)
        weigh(1, s1)
        scores(2, s0)

        weigh(2, s0)
        scores(3, s1)
        weigh(3, s1)

        @pl.when(c == 0)
        def _():
            for line in p2:
                for cp in line:
                    cp.wait()
            for cp in ref_swap:
                cp.start()

        return 0

    lax.fori_loop(0, 3, attend, 0)
    relay.wait_recv()
    project(3)
    local[12].wait()
    wout = wso[pl.ds(pl.multiple_of(OWN * core, 16), OWN), :]
    swaps = [
        remote(psend.at[pl.ds(lo, n)], precv.at[pl.ds(lo, n)], ps.at[j], pr.at[j], sib)
        for j, (lo, n) in enumerate(PARTS)
    ]
    few = LAST // FRAMES
    tall = FRAMES * 16

    def pack(values):
        slot_row = lax.broadcasted_iota(jnp.int32, (tall, LAST), 0)
        cell = lax.broadcasted_iota(jnp.int32, (tall, LAST), 1)
        total = None
        for t in range(C // 128):
            want = slot_row - t * few
            hit = jnp.logical_and(want % 16 < few, cell == (slot_row // 16) * few + want % 16)
            hit = jnp.logical_and(hit, want % 16 == slot_row % 16 - t * few)
            term = dot(jnp.where(hit, 1.0, 0.0).astype(BF), values[:, 128 * t : 128 * (t + 1)])
            total = term if total is None else total + term
        return total.reshape(FRAMES, 16, 128).astype(BF)

    def unpack(slots):
        slot_row = lax.broadcasted_iota(jnp.int32, (LAST, tall), 1)
        cell = lax.broadcasted_iota(jnp.int32, (LAST, tall), 0)
        flat = slots.reshape(tall, 128)
        return jnp.concatenate(
            [
                dot(
                    jnp.where(
                        slot_row == (cell // few) * 16 + t * few + cell % few, 1.0, 0.0
                    ).astype(BF),
                    flat,
                )
                for t in range(C // 128)
            ],
            axis=1,
        )

    hops = sorted(
        ((dx, dz, dy) for dx in range(4) for dz in range(2) for dy in range(4) if dx + dz + dy),
        key=lambda d: -(min(d[0], 4 - d[0]) + d[1] + min(d[2], 4 - d[2])),
    )
    zl = (f // 4) % 2
    rounds = [lax.rem(x + dx, 4) * 8 + lax.rem(zl + dz, 2) * 4 + lax.rem(y + dy, 4) for dx, dz, dy in hops]

    def to_all(src, dst, send, recv):
        for peer in rounds:
            remote(src.at[peer], dst.at[f], send, recv, (peer, s)).start()
        dst[f] = src[f]

    def from_all(src, dst, send, recv):
        every = pl.ds(0, FRAMES - 1)
        remote(src.at[every], dst.at[every], send, recv, sib).wait()

    def out_project(j):
        lo, n = PARTS[j]
        at = slice(2 * lo, 2 * lo + 2 * n)
        for h in range(MINE):
            qt[h * D : (h + 1) * D, at] = (acc[h, :D, at] / acc[h, D : D + 1, at]).astype(BF)
        part[at, :] = dot_tn(qt[:, at], wout)
        psend[lo : lo + n, :] = part[2 * lo + n : 2 * lo + 2 * n, :].astype(BF)
        swaps[j].start()

    def depart(j):
        lo, n = PARTS[j]
        swaps[j].wait()
        at = slice(lo, lo + n)
        after = mid[at, :] + part[2 * lo : 2 * lo + n, :] + precv[at, :].astype(F32)
        if n < WIDE:
            lsend[...] = pack(after.astype(BF))
            to_all(lsend, lrecv, a_s.at[j], a_r.at[j])
        else:
            asend[j] = after.reshape(FRAMES, SLOT, C).astype(BF)
            to_all(asend.at[j], arecv.at[j], a_s.at[j], a_r.at[j])

    items = [(j, h) for j in range(CHUNKS) for h in range(MINE)]

    def span(j):
        return 2 * PARTS[j][0], 2 * PARTS[j][1]

    scores(0, s0, *span(0))
    for i, (j, h) in enumerate(items):
        weigh(h, (s0, s1)[i % 2], *span(j))
        if i + 1 < len(items):
            jn, hn = items[i + 1]
            scores(hn, (s0, s1)[(i + 1) % 2], *span(jn))
        if h == MINE - 1:
            out_project(j)
        if j > 0 and h == 1:
            depart(j - 1)
    for i in range(13, len(local)):
        local[i].wait()
    depart(CHUNKS - 1)

    to_sib.wait_send()
    to_far.wait_send()
    relay.wait_send()
    for cp in ref_swap:
        cp.wait_send()

    gain_time = norm_time[...].reshape(1, C)
    zero = jnp.zeros((SLOT, C), F32)
    def same_cell(n, cells):
        return (
            lax.broadcasted_iota(jnp.int32, (n, n), 0) % cells
            == lax.broadcasted_iota(jnp.int32, (n, n), 1) % cells
        )

    def through_time(block, n, same):
        timed = (block + dot(tgrid[:n, :], wc[0])).astype(BF).astype(F32)
        tn = layer_norm(timed, gain_time).astype(BF)
        q = (dot(tn, wc[1, 0 * C : 1 * C, :]) * SCALE).astype(BF)
        k = dot(tn, wc[1, 1 * C : 2 * C, :]).astype(BF)
        v = dot(tn, wc[1, 2 * C : 3 * C, :]).astype(BF)
        for h in range(HEADS):
            lo, hi = (h * D) // 128 * 128, -(-((h + 1) * D) // 128) * 128
            ln = lax.broadcasted_iota(jnp.int32, (1, hi - lo), 1) + lo
            inside = jnp.logical_and(ln >= h * D, ln < (h + 1) * D)
            qh = q[:, lo:hi] * jnp.where(inside, 1.0, 0.0).astype(BF)
            sc = jnp.where(same, dot_nt(qh, k[:, lo:hi]), -1e30)
            e = jnp.exp2(sc - jnp.max(sc, axis=1, keepdims=True))
            total = jnp.sum(e, axis=1, keepdims=True)
            o = dot(e.astype(BF), v[:, lo:hi]) / total
            if h == 0:
                tatt[:n, lo:hi] = o
            else:
                tatt[:n, lo:hi] = jnp.where(inside, o, tatt[:n, lo:hi])
        return timed + dot(tatt[:n, :].astype(BF), wc[2, :C, :])

    all_rows = same_cell(WIDE, SLOT)

    def full_part(j, _):
        from_all(asend.at[j], arecv.at[j], a_s.at[j], a_r.at[j])
        block = arecv[j].astype(F32).reshape(WIDE, C)
        tgrid[:, :C] = jnp.concatenate([zero, block[:-SLOT]], axis=0).astype(BF)
        tgrid[:, C : 2 * C] = block.astype(BF)
        tgrid[:, 2 * C :] = jnp.concatenate([block[SLOT:], zero], axis=0).astype(BF)
        res = through_time(block, WIDE, all_rows)
        asend[j] = res.reshape(FRAMES, SLOT, C).astype(BF)
        to_all(asend.at[j], brecv.at[j], b_s.at[j], b_r.at[j])
        return 0

    lax.fori_loop(0, CHUNKS - 1, full_part, 0)

    last = CHUNKS - 1
    at_row = lax.broadcasted_iota(jnp.int32, (LAST, LAST), 0)
    from_row = lax.broadcasted_iota(jnp.int32, (LAST, LAST), 1)
    from_all(lsend, lrecv, a_s.at[last], a_r.at[last])
    block = unpack(lrecv[...])
    tgrid[:LAST, C : 2 * C] = block.astype(BF)
    for t in (0, 2):
        near = jnp.where(from_row == at_row + (t - 1) * few, 1.0, 0.0).astype(BF)
        tgrid[:LAST, t * C : (t + 1) * C] = dot(near, block.astype(BF)).astype(BF)
    res = through_time(block, LAST, same_cell(LAST, few))
    lsend[...] = pack(res.astype(BF))
    to_all(lsend, lback, b_s.at[last], b_r.at[last])

    done = [
        pltpu.make_async_copy(oblk.at[pl.ds(lo, n)], out.at[pl.ds(lo, n)], lsem.at[j])
        for j, (lo, n) in enumerate(PARTS)
    ]
    for j, (lo, n) in enumerate(PARTS):
        if n < WIDE:
            from_all(lsend, lback, b_s.at[j], b_r.at[j])
            got = unpack(lback[...])
        else:
            from_all(asend.at[j], brecv.at[j], b_s.at[j], b_r.at[j])
            got = brecv[j].astype(F32).reshape(WIDE, C)
        oblk[lo : lo + n, :] = got.astype(BF)
        done[j].start()
    for cp in done:
        cp.wait()


def block(
    frames_in, reference_rows, norm_conv, conv_weight, norm_attn, spatial_qkv, spatial_out,
    time_weight, norm_time, temporal_qkv, temporal_out,
):
    hbm = pl.BlockSpec(memory_space=pl.ANY)
    vm = pl.BlockSpec(memory_space=pltpu.VMEM)
    v = pltpu.VMEM
    dma = pltpu.SemaphoreType.DMA
    scratch = [
        v((CELLS, C), BF), v((3, 3 * C, C), BF), v((3, C, C), BF), v((C, C), BF),
        v((96, C), BF), v((96, C), BF), v((CELLS + 2 * ROWS, 3 * C), BF), v((CELLS, C), F32),
        v((8, 18, C), BF), v((4, 2, 4, 144, C), BF), v((OWN, C), BF), v((OWN, C), BF),
        v((C, MINE * 128), BF), v((OWN, CHIP), BF), v((MINE, CHIP, 128), BF), v((MINE, 96, CHIP), BF),
        v((MINE, 96, CHIP), F32), v((MINE, 1, CHIP), F32), v((MINE, 1, CHIP), F32),
        v((CHIP, CHIP), F32), v((CHIP, CHIP), F32),
        v((CHIP, C), F32), v((CELLS, C), BF), v((CELLS, C), BF),
        v((CHUNKS - 1, FRAMES, SLOT, C), BF), v((CHUNKS - 1, FRAMES, SLOT, C), BF),
        v((CHUNKS - 1, FRAMES, SLOT, C), BF),
        v((FRAMES, 16, 128), BF), v((FRAMES, 16, 128), BF), v((FRAMES, 16, 128), BF),
        v((WIDE, 3 * C), BF), v((WIDE, C), F32), v((CELLS, C), BF),
        dma((20,)), dma((2,)), dma((2,)), dma((7,)), dma((7,)),
        dma((3,)), dma((3,)), dma((4, 3)), dma((4, 3)), dma((5,)), dma((5,)), dma((3,)), dma((3,)),
        dma((CHUNKS,)), dma((CHUNKS,)), dma((CHUNKS,)), dma((CHUNKS,)),
    ]
    cells = frames_in.transpose(0, 2, 1, 3).reshape(CELLS, C)
    res = pl.pallas_call(
        kernel,
        out_shape=jax.ShapeDtypeStruct((CELLS, C), BF),
        in_specs=[hbm, hbm, vm, hbm, vm, hbm, hbm, hbm, vm, hbm, hbm],
        out_specs=hbm,
        scratch_shapes=scratch,
        compiler_params=pltpu.CompilerParams(
            collective_id=0, has_side_effects=True, vmem_limit_bytes=62 * 2**20
        ),
    )(
        cells, reference_rows, norm_conv, conv_weight, norm_attn, spatial_qkv, spatial_out,
        time_weight, norm_time, temporal_qkv, temporal_out,
    )
    return res.reshape(1, W, ROWS, C).transpose(0, 2, 1, 3)


def solution(mesh):
    rep = P()
    in_specs = (P("frame", "sp", None, None), P(("frame", "sp"), None)) + (rep,) * 9
    return jax.shard_map(
        block, mesh=mesh, in_specs=in_specs, out_specs=P("frame", "sp", None, None), check_vma=False
    )
```

```python
import functools

import jax
import jax.numpy as jnp
from jax import lax
from jax.experimental import pallas as pl
from jax.experimental.pallas import tpu as pltpu
from jax.sharding import PartitionSpec as P

MESH = pl.DeviceIdType.MESH
BF = jnp.bfloat16
F32 = jnp.float32
C = 640
HEADS = 8
D = 80
MINE = 4
OWN = MINE * D
ROWS = 16
W = 36
CELLS = 576
CHIP = 1152
FRAMES = 32
SLOT = 8
WIDE = FRAMES * SLOT
PARTS = ((0, 256), (256, 256), (512, 64))
CHUNKS = len(PARTS)
LAST = PARTS[2][1]
SCALE = (D ** -0.5) * 1.4426950408889634


def dot(a, b):
    return jnp.dot(a, b, preferred_element_type=F32)


def dot_nt(a, b):
    return lax.dot_general(a, b, (((1,), (1,)), ((), ())), preferred_element_type=F32)


def dot_tn(a, b):
    return lax.dot_general(a, b, (((0,), (0,)), ((), ())), preferred_element_type=F32)


def layer_norm(values, gain):
    mean = jnp.mean(values, axis=-1, keepdims=True)
    centred = values - mean
    spread = jnp.mean(centred * centred, axis=-1, keepdims=True)
    return centred * lax.rsqrt(spread + 1e-05) * gain


def kernel(
    frames, refs, norm_conv, conv_w, norm_attn, sqkv, sout, time_w, norm_time, tqkv, tout,
    out,
    xin, wc, wsq, wso,
    rims, rimr, grid, mid,
    rblk, allx, wqt, wvt, wkp, qt, kk, vt, acc, mx, al, s0, s1,
    part, psend, precv,
    asend, arecv, brecv, lsend, lrecv, lback, into, outof, tgrid, tatt, oblk,
    lsem, hs, hr, cs, cr, p1s, p1r, p2s, p2r, xs, xr, ps, pr, a_s, a_r, b_s, b_r,
):
    f = lax.axis_index("frame")
    s = lax.axis_index("sp")
    x = f // 8
    y = f % 4
    z = (s // 2) * 2 + (f // 4) % 2
    core = s % 2
    zc = z * 2 + core

    def dev(px, py, pz, pc):
        px, py, pz = lax.rem(px, 4), lax.rem(py, 4), lax.rem(pz, 4)
        return ((px * 2 + pz % 2) * 4 + py, (pz // 2) * 2 + pc)

    sib = (f, (s // 2) * 2 + 1 - core)
    far = (f, lax.rem(s + 2, 4))

    loads = [
        (frames, xin),
        (refs, rblk.at[zc]),
        (sqkv, wsq),
    ]
    loads += [(conv_w.at[a, b], wc.at[b, pl.ds(a * C, C)]) for b in range(3) for a in range(3)]
    loads += [(sout, wso)]
    loads += [(time_w.at[a], wc.at[0, pl.ds(a * C, C)]) for a in range(3)]
    loads += [(tqkv.at[a], wc.at[1, pl.ds(a * C, C)]) for a in range(3)]
    loads += [(tout, wc.at[2, pl.ds(0, C)])]
    local = [pltpu.make_async_copy(a, b, lsem.at[i]) for i, (a, b) in enumerate(loads)]
    for cp in local[:13]:
        cp.start()

    bar = pltpu.get_barrier_semaphore()
    column = [(dz, dc) for dz in range(4) for dc in range(2) if dz + dc > 0]

    def col_dev(dz, dc):
        return dev(x, y, z + dz, lax.rem(core + dc, 2))

    others = [(dz, dc) for dz, dc in column if not (dz == 0 and dc == 0)]
    for dz, dc in others:
        pl.semaphore_signal(bar, inc=1, device_id=col_dev(dz, dc), device_id_type=MESH)

    for i in (1, 2, 3):
        pl.semaphore_signal(bar, inc=1, device_id=dev(x + i, y, z, core), device_id_type=MESH)
        pl.semaphore_signal(bar, inc=1, device_id=dev(x, y + i, z, core), device_id_type=MESH)

    local[0].wait()
    rim_row = lax.broadcasted_iota(jnp.int32, (96, CELLS), 0)
    rim_cell = lax.broadcasted_iota(jnp.int32, (96, CELLS), 1)
    rim = jnp.where(
        rim_cell == jnp.where(rim_row < 48, rim_row * ROWS, (rim_row - 48) * ROWS + ROWS - 1), 1.0, 0.0
    ).astype(BF)
    rims[...] = dot(rim, xin[...]).astype(BF)

    local[2].wait()
    pick = (
        lax.broadcasted_iota(jnp.int32, (OWN, C), 1)
        == lax.broadcasted_iota(jnp.int32, (OWN, C), 0) + OWN * core
    ).astype(F32).astype(BF)
    wqt[...] = dot_nt(pick, wsq[0]).astype(BF)
    wvt[...] = dot_nt(pick, wsq[2]).astype(BF)
    lane = lax.broadcasted_iota(jnp.int32, (C, MINE * 128), 1)
    row = lax.broadcasted_iota(jnp.int32, (C, MINE * 128), 0)
    spread = jnp.where(
        jnp.logical_and(lane % 128 < D, row == OWN * core + (lane // 128) * D + lane % 128), 1.0, 0.0
    ).astype(BF)
    wkp[...] = dot(wsq[1], spread).astype(BF)
    vt[:, D:, :] = jnp.where(
        lax.broadcasted_iota(jnp.int32, (MINE, 16, CHIP), 1) == 0, 1.0, 0.0
    ).astype(BF)

    def remote(src, dst, send, recv, to):
        return pltpu.make_async_remote_copy(
            src_ref=src, dst_ref=dst, send_sem=send, recv_sem=recv, device_id=to, device_id_type=MESH
        )

    gain_conv = norm_conv[...].reshape(1, C)

    def activated(v):
        v = layer_norm(v.astype(F32), gain_conv)
        return v / (1.0 + jnp.exp(-v))

    nothing = jnp.zeros((8, C), F32)

    def activate(k, _):
        v = activated(xin[pl.ds(pl.multiple_of(64 * k, 16), 64), :])
        for i in range(4):
            at = pl.multiple_of(128 * k + 32 * i, 8)
            part[pl.ds(at, 8), :] = nothing
            part[pl.ds(at + 8, ROWS), :] = v[ROWS * i : ROWS * (i + 1)]
            part[pl.ds(at + 24, 8), :] = nothing
        return 0

    lax.fori_loop(0, CELLS // 64, activate, 0)

    grid[:ROWS, :] = jnp.zeros((ROWS, 3 * C), BF)
    grid[CELLS + ROWS :, :] = jnp.zeros((ROWS, 3 * C), BF)
    for k in range(W):
        for a in range(3):
            grid[ROWS * (k + 1) : ROWS * (k + 2), a * C : (a + 1) * C] = part[
                32 * k + 7 + a : 32 * k + 7 + a + ROWS, :
            ].astype(BF)
    for i in range(3, 12):
        local[i].wait()

    def conv_tap(b):
        return dot(grid[ROWS * b : ROWS * b + CELLS, :], wc[b])

    few = LAST // FRAMES
    slot_row = lax.broadcasted_iota(jnp.int32, (FRAMES * 16, LAST), 0)
    cell = lax.broadcasted_iota(jnp.int32, (FRAMES * 16, LAST), 1)
    slot_col = lax.broadcasted_iota(jnp.int32, (LAST, FRAMES * 16), 1)
    cell_row = lax.broadcasted_iota(jnp.int32, (LAST, FRAMES * 16), 0)
    for t in range(C // 128):
        into[t] = jnp.where(
            slot_row == (cell // few) * 16 + t * few + cell % few, 1.0, 0.0
        ).astype(BF)
        outof[t] = jnp.where(
            slot_col == (cell_row // few) * 16 + t * few + cell_row % few, 1.0, 0.0
        ).astype(BF)

    pl.semaphore_wait(bar, 13)
    up = remote(
        rims.at[pl.ds(0, 48)], rimr.at[pl.ds(48, 48)], hs.at[0], hr.at[0], (f, jnp.maximum(s - 1, 0))
    )
    down = remote(
        rims.at[pl.ds(48, 48)], rimr.at[pl.ds(0, 48)], hs.at[1], hr.at[1], (f, jnp.minimum(s + 1, 3))
    )

    @pl.when(s > 0)
    def _():
        up.start()

    @pl.when(s < 3)
    def _():
        down.start()

    col = [
        remote(rblk.at[zc], rblk.at[zc], cs.at[i], cr.at[i], col_dev(dz, dc))
        for i, (dz, dc) in enumerate(column)
    ]
    local[1].wait()
    for cp in col:
        cp.start()


    mid[...] = conv_tap(0)
    mid[...] += conv_tap(1)
    mid[...] += conv_tap(2)

    for cp in col:
        cp.wait()
    for i in range(8):
        tatt[pl.ds(18 * i, 18), :] = rblk[i].astype(F32)
    mine = jnp.int32(1) + x // 2
    allx[mine, lax.rem(x, 2), y] = tatt[:144, :].astype(BF)


    def share(first, count):
        return pl.ds(pl.multiple_of(first, 16), count)

    half = share(64 * core, 80)

    def line_one(i):
        return dev(x + i * (1 - core), y + i * core, z, core)

    def line_two(i):
        return dev(x + i * core, y + i * (1 - core), z, core)

    def home(i):
        px, py = lax.rem(x + 4 - i * (1 - core), 4), lax.rem(y + 4 - i * core, 4)
        return allx.at[1 + px // 2, lax.rem(px, 2), py, half]

    p1 = [remote(home(0), home(0), p1s.at[i - 1], p1r.at[i - 1], line_one(i)) for i in (1, 2, 3)]
    p2 = [
        [
            remote(home(k), home(k), p2s.at[k, i - 1], p2r.at[k, i - 1], line_two(i))
            for i in (1, 2, 3)
        ]
        for k in range(4)
    ]
    for cp in p1 + p2[0]:
        cp.start()

    def patch(tap, first, values):
        rim = activated(values).astype(BF)
        for b in range(3):
            part[64 * b : 64 * b + 8, :] = nothing
            part[64 * b + 8 : 64 * b + 56, :] = dot(rim, wc[b, tap * C : (tap + 1) * C, :])
        part[192 : 192 + W, :] = part[7 : 7 + W, :] + part[72 : 72 + W, :] + part[137 : 137 + W, :]
        for k in range(W):
            mid[ROWS * k + first : ROWS * k + first + 1, :] += part[192 + k : 193 + k, :]

    @pl.when(s > 0)
    def _():
        down.wait_recv()
        patch(0, 0, rimr[:48])

    @pl.when(s < 3)
    def _():
        up.wait_recv()
        patch(2, ROWS - 1, rimr[48:])

    @pl.when(s > 0)
    def _():
        up.wait_send()

    @pl.when(s < 3)
    def _():
        down.wait_send()

    for cp in local[13:]:
        cp.start()
    gain_attn = norm_attn[...].reshape(1, C)

    def settle(k, _):
        at = pl.ds(pl.multiple_of(144 * k, 16), 144)
        middle = (xin[at, :].astype(F32) + mid[at, :]).astype(BF).astype(F32)
        mid[at, :] = middle
        allx[0, 0, k] = layer_norm(middle, gain_attn).astype(BF)
        return 0

    lax.fori_loop(0, 4, settle, 0)

    to_sib = remote(allx.at[0, 0], allx.at[0, 1], xs.at[0], xr.at[0], sib)
    to_far = remote(allx.at[0, 0], allx.at[3, 0], xs.at[1], xr.at[1], far)
    to_far.start()
    to_sib.start()
    relay = remote(allx.at[3, 0], allx.at[3, 1], xs.at[2], xr.at[2], sib)
    ref_swap = [
        remote(
            allx.at[k, :, :, share(80 * core, 64)], allx.at[k, :, :, share(80 * core, 64)],
            xs.at[2 + k], xr.at[2 + k], sib,
        )
        for k in (1, 2)
    ]

    acc[...] = jnp.zeros_like(acc)
    mx[...] = jnp.full_like(mx, -1e30)
    to_sib.wait_recv()
    own, next_door = allx[0, 0].reshape(CELLS, C), allx[0, 1].reshape(CELLS, C)
    asking = jnp.concatenate(
        [cells[lo : lo + n] for lo, n in PARTS for cells in (own, next_door)], axis=0
    )
    qall = dot_nt(wqt[...], asking) * SCALE
    qt[...] = qall.astype(BF)
    for i in range(3):
        p1[i].wait()
        for cp in p2[i + 1]:
            cp.start()

    def scores(h, sref, lo=0, n=CHIP):
        at = slice(lo, lo + n)
        sc = dot(kk[h][:, :D], qt[h * D : (h + 1) * D, at])
        sref[:, :n] = sc
        old = mx[h, :, at]
        new = jnp.maximum(old, jnp.max(sc, axis=0, keepdims=True))
        mx[h, :, at] = new
        al[h, :, at] = jnp.exp2(old - new)

    def weigh(h, sref, lo=0, n=CHIP):
        at = slice(lo, lo + n)
        p = jnp.exp2(sref[:, :n] - mx[h, :, at]).astype(BF)
        acc[h, :, at] = acc[h, :, at] * al[h, :, at] + dot(vt[h], p)

    def project(c):
        rows = allx[c].reshape(CHIP, C)
        keys = dot(rows, wkp[...])
        vals = dot_nt(wvt[...], rows)
        for h in range(MINE):
            kk[h] = keys[:, h * 128 : (h + 1) * 128].astype(BF)
            vt[h, :D, :] = vals[h * D : (h + 1) * D, :].astype(BF)

    def attend(c, _):
        @pl.when(c == 1)
        def _():
            ref_swap[0].wait_recv()

        @pl.when(c == 2)
        def _():
            ref_swap[1].wait_recv()
            to_far.wait_recv()
            relay.start()

        project(c)
        scores(0, s0)
        weigh(0, s0)
        scores(1, s1)
        weigh(1, s1)
        scores(2, s0)

        weigh(2, s0)
        scores(3, s1)
        weigh(3, s1)

        @pl.when(c == 0)
        def _():
            for line in p2:
                for cp in line:
                    cp.wait()
            for cp in ref_swap:
                cp.start()

        return 0

    lax.fori_loop(0, 3, attend, 0)
    relay.wait_recv()
    project(3)
    local[12].wait()
    wout = wso[pl.ds(pl.multiple_of(OWN * core, 16), OWN), :]
    swaps = [
        remote(psend.at[pl.ds(lo, n)], precv.at[pl.ds(lo, n)], ps.at[j], pr.at[j], sib)
        for j, (lo, n) in enumerate(PARTS)
    ]
    tall = FRAMES * 16

    def pack(values):
        total = dot(into[0], values[:, :128])
        for t in range(1, C // 128):
            total += dot(into[t], values[:, 128 * t : 128 * (t + 1)])
        return total.reshape(FRAMES, 16, 128).astype(BF)

    def unpack(slots):
        flat = slots.reshape(tall, 128)
        return jnp.concatenate([dot(outof[t], flat) for t in range(C // 128)], axis=1)

    hops = sorted(
        ((dx, dz, dy) for dx in range(4) for dz in range(2) for dy in range(4) if dx + dz + dy),
        key=lambda d: -(min(d[0], 4 - d[0]) + d[1] + min(d[2], 4 - d[2])),
    )
    zl = (f // 4) % 2
    rounds = [lax.rem(x + dx, 4) * 8 + lax.rem(zl + dz, 2) * 4 + lax.rem(y + dy, 4) for dx, dz, dy in hops]

    def to_all(src, dst, send, recv):
        for peer in rounds:
            remote(src.at[peer], dst.at[f], send, recv, (peer, s)).start()
        dst[f] = src[f]

    def from_all(src, dst, send, recv):
        every = pl.ds(0, FRAMES - 1)
        remote(src.at[every], dst.at[every], send, recv, sib).wait()

    def out_project(j):
        lo, n = PARTS[j]
        at = slice(2 * lo, 2 * lo + 2 * n)
        for h in range(MINE):
            qt[h * D : (h + 1) * D, at] = (acc[h, :D, at] / acc[h, D : D + 1, at]).astype(BF)
        part[at, :] = dot_tn(qt[:, at], wout)
        psend[lo : lo + n, :] = part[2 * lo + n : 2 * lo + 2 * n, :].astype(BF)
        swaps[j].start()

    def depart(j):
        lo, n = PARTS[j]
        swaps[j].wait()
        at = slice(lo, lo + n)
        after = mid[at, :] + part[2 * lo : 2 * lo + n, :] + precv[at, :].astype(F32)
        if n < WIDE:
            lsend[...] = pack(after.astype(BF))
            to_all(lsend, lrecv, a_s.at[j], a_r.at[j])
        else:
            asend[j] = after.reshape(FRAMES, SLOT, C).astype(BF)
            to_all(asend.at[j], arecv.at[j], a_s.at[j], a_r.at[j])

    items = [(j, h) for j in range(CHUNKS) for h in range(MINE)]

    def span(j):
        return 2 * PARTS[j][0], 2 * PARTS[j][1]

    scores(0, s0, *span(0))
    for i, (j, h) in enumerate(items):
        weigh(h, (s0, s1)[i % 2], *span(j))
        if i + 1 < len(items):
            jn, hn = items[i + 1]
            scores(hn, (s0, s1)[(i + 1) % 2], *span(jn))
        if h == MINE - 1:
            out_project(j)
        if j > 0 and h == 1:
            depart(j - 1)
    for i in range(13, len(local)):
        local[i].wait()
    depart(CHUNKS - 1)

    to_sib.wait_send()
    to_far.wait_send()
    relay.wait_send()
    for cp in ref_swap:
        cp.wait_send()

    gain_time = norm_time[...].reshape(1, C)
    zero = jnp.zeros((SLOT, C), F32)
    def same_cell(n, cells):
        return (
            lax.broadcasted_iota(jnp.int32, (n, n), 0) % cells
            == lax.broadcasted_iota(jnp.int32, (n, n), 1) % cells
        )

    def through_time(block, n, same):
        timed = (block + dot(tgrid[:n, :], wc[0])).astype(BF).astype(F32)
        tn = layer_norm(timed, gain_time).astype(BF)
        q = (dot(tn, wc[1, 0 * C : 1 * C, :]) * SCALE).astype(BF)
        k = dot(tn, wc[1, 1 * C : 2 * C, :]).astype(BF)
        v = dot(tn, wc[1, 2 * C : 3 * C, :]).astype(BF)
        for h in range(HEADS):
            lo, hi = (h * D) // 128 * 128, -(-((h + 1) * D) // 128) * 128
            ln = lax.broadcasted_iota(jnp.int32, (1, hi - lo), 1) + lo
            inside = jnp.logical_and(ln >= h * D, ln < (h + 1) * D)
            qh = q[:, lo:hi] * jnp.where(inside, 1.0, 0.0).astype(BF)
            sc = jnp.where(same, dot_nt(qh, k[:, lo:hi]), -1e30)
            e = jnp.exp2(sc - jnp.max(sc, axis=1, keepdims=True))
            total = jnp.sum(e, axis=1, keepdims=True)
            o = dot(e.astype(BF), v[:, lo:hi]) / total
            if h == 0:
                tatt[:n, lo:hi] = o
            else:
                tatt[:n, lo:hi] = jnp.where(inside, o, tatt[:n, lo:hi])
        return timed + dot(tatt[:n, :].astype(BF), wc[2, :C, :])

    all_rows = same_cell(WIDE, SLOT)

    def full_part(j, _):
        from_all(asend.at[j], arecv.at[j], a_s.at[j], a_r.at[j])
        block = arecv[j].astype(F32).reshape(WIDE, C)
        tgrid[:, :C] = jnp.concatenate([zero, block[:-SLOT]], axis=0).astype(BF)
        tgrid[:, C : 2 * C] = block.astype(BF)
        tgrid[:, 2 * C :] = jnp.concatenate([block[SLOT:], zero], axis=0).astype(BF)
        res = through_time(block, WIDE, all_rows)
        asend[j] = res.reshape(FRAMES, SLOT, C).astype(BF)
        to_all(asend.at[j], brecv.at[j], b_s.at[j], b_r.at[j])
        return 0

    lax.fori_loop(0, CHUNKS - 1, full_part, 0)

    last = CHUNKS - 1
    at_row = lax.broadcasted_iota(jnp.int32, (LAST, LAST), 0)
    from_row = lax.broadcasted_iota(jnp.int32, (LAST, LAST), 1)
    from_all(lsend, lrecv, a_s.at[last], a_r.at[last])
    block = unpack(lrecv[...])
    tgrid[:LAST, C : 2 * C] = block.astype(BF)
    for t in (0, 2):
        near = jnp.where(from_row == at_row + (t - 1) * few, 1.0, 0.0).astype(BF)
        tgrid[:LAST, t * C : (t + 1) * C] = dot(near, block.astype(BF)).astype(BF)
    res = through_time(block, LAST, same_cell(LAST, few))
    lsend[...] = pack(res.astype(BF))
    to_all(lsend, lback, b_s.at[last], b_r.at[last])

    done = [
        pltpu.make_async_copy(oblk.at[pl.ds(lo, n)], out.at[pl.ds(lo, n)], lsem.at[j])
        for j, (lo, n) in enumerate(PARTS)
    ]
    for j, (lo, n) in enumerate(PARTS):
        if n < WIDE:
            from_all(lsend, lback, b_s.at[j], b_r.at[j])
            got = unpack(lback[...])
        else:
            from_all(asend.at[j], brecv.at[j], b_s.at[j], b_r.at[j])
            got = brecv[j].astype(F32).reshape(WIDE, C)
        oblk[lo : lo + n, :] = got.astype(BF)
        done[j].start()
    for cp in done:
        cp.wait()


def block(
    frames_in, reference_rows, norm_conv, conv_weight, norm_attn, spatial_qkv, spatial_out,
    time_weight, norm_time, temporal_qkv, temporal_out,
):
    hbm = pl.BlockSpec(memory_space=pl.ANY)
    vm = pl.BlockSpec(memory_space=pltpu.VMEM)
    v = pltpu.VMEM
    dma = pltpu.SemaphoreType.DMA
    scratch = [
        v((CELLS, C), BF), v((3, 3 * C, C), BF), v((3, C, C), BF), v((C, C), BF),
        v((96, C), BF), v((96, C), BF), v((CELLS + 2 * ROWS, 3 * C), BF), v((CELLS, C), F32),
        v((8, 18, C), BF), v((4, 2, 4, 144, C), BF), v((OWN, C), BF), v((OWN, C), BF),
        v((C, MINE * 128), BF), v((OWN, CHIP), BF), v((MINE, CHIP, 128), BF), v((MINE, 96, CHIP), BF),
        v((MINE, 96, CHIP), F32), v((MINE, 1, CHIP), F32), v((MINE, 1, CHIP), F32),
        v((CHIP, CHIP), F32), v((CHIP, CHIP), F32),
        v((CHIP, C), F32), v((CELLS, C), BF), v((CELLS, C), BF),
        v((CHUNKS - 1, FRAMES, SLOT, C), BF), v((CHUNKS - 1, FRAMES, SLOT, C), BF),
        v((CHUNKS - 1, FRAMES, SLOT, C), BF),
        v((FRAMES, 16, 128), BF), v((FRAMES, 16, 128), BF), v((FRAMES, 16, 128), BF),
        v((C // 128, FRAMES * 16, LAST), BF), v((C // 128, LAST, FRAMES * 16), BF),
        v((WIDE, 3 * C), BF), v((WIDE, C), F32), v((CELLS, C), BF),
        dma((20,)), dma((2,)), dma((2,)), dma((7,)), dma((7,)),
        dma((3,)), dma((3,)), dma((4, 3)), dma((4, 3)), dma((5,)), dma((5,)), dma((3,)), dma((3,)),
        dma((CHUNKS,)), dma((CHUNKS,)), dma((CHUNKS,)), dma((CHUNKS,)),
    ]
    cells = frames_in.transpose(0, 2, 1, 3).reshape(CELLS, C)
    res = pl.pallas_call(
        kernel,
        out_shape=jax.ShapeDtypeStruct((CELLS, C), BF),
        in_specs=[hbm, hbm, vm, hbm, vm, hbm, hbm, hbm, vm, hbm, hbm],
        out_specs=hbm,
        scratch_shapes=scratch,
        compiler_params=pltpu.CompilerParams(
            collective_id=0, has_side_effects=True, vmem_limit_bytes=62 * 2**20
        ),
    )(
        cells, reference_rows, norm_conv, conv_weight, norm_attn, spatial_qkv, spatial_out,
        time_weight, norm_time, temporal_qkv, temporal_out,
    )
    return res.reshape(1, W, ROWS, C).transpose(0, 2, 1, 3)


def solution(mesh):
    rep = P()
    in_specs = (P("frame", "sp", None, None), P(("frame", "sp"), None)) + (rep,) * 9
    return jax.shard_map(
        block, mesh=mesh, in_specs=in_specs, out_specs=P("frame", "sp", None, None), check_vma=False
    )
```
